128 devices in a mesh: member: 4 (over y_hi, core), band: 32 (over y_lo, x, z).
Axes of the slice: x: 4, y: 4 (y_hi: 2, y_lo: 2; y = y_hi * 2 + y_lo), z: 4, core: 2. Of those that a mesh axis runs over, the one named last changes fastest.
Arguments:
- fields: float32 [32, 2, 2048, 2048], P('member', None, 'band'), may hold values from -48 to 48
- observed: float32 [2, 512, 512], P(None, 'band'), may hold values from -2.4 to 2.4
Outputs:
- field_gradient: float32 [32, 2, 2048, 2048], P('member', None, 'band')
The draws below stay inside these ranges and needn't reach their ends.
All inputs are finite; a program needn't handle non-finite values.
Results may differ from the reference program's by a relative error of at most 0.00013.
Values sent between devices are 32-bit elements; how exact they have to be, the bound alone decides.
No kernel may reach another device: no remote copies, remote signals or barrier semaphores. Data moves between devices by JAX's collectives and lax.ppermute only.
A program may use at most 64 MiB of HBM per device.

```python
import jax
import jax.numpy as jnp
from jax import lax

ENS = 32
VARS = 2
RADIUS = 16
LON = 2048
LAT = 2048


def steps_of(key, dims, split, low, top_value):
    gain, own = 1.0, jax.random.fold_in(key, 6)
    for position, parts in split:
        steps = jnp.exp(jax.random.uniform(jax.random.fold_in(own, position), (parts,), jnp.float32, low / len(split), top_value / len(split)))
        gain = gain * jnp.repeat(steps, dims[position] // parts).reshape([-1 if axis == position else 1 for axis in range(len(dims))])
    return gain


def scatter_about(key, extent, deviation, limit, shards=(), dtype=jnp.bfloat16):
    factor_of = steps_of(key, extent, shards, -0.22, 0.18) if shards else 1.0
    drawn = jax.random.normal(key, extent, jnp.float32) * deviation * factor_of
    return jnp.minimum(jnp.maximum(drawn, -limit), limit).astype(dtype)


def setup_inputs(seed: int = 0) -> dict:
    keys = jax.random.split(jax.random.key(seed), 3)
    fields = scatter_about(keys[0], (ENS, VARS, LAT, LON), 8.0, 48.0, ((0, 4), (2, 32)), jnp.float32)
    observed = scatter_about(keys[1], (VARS, LAT // 4, LON // 4), 0.4, 2.4, ((1, 32),), jnp.float32)
    return dict(fields=fields, observed=observed)


smooth_sigma = 6.0
huber_width = 0.05

def kernel(offset):
    spot = offset.astype(jnp.float32)
    tap_ids = jnp.arange(-RADIUS, RADIUS + 1).astype(jnp.float32)
    normaliser = jnp.sum(jnp.exp(-tap_ids * tap_ids / (2.0 * smooth_sigma * smooth_sigma)))
    inside = jnp.abs(spot) <= RADIUS
    return jnp.where(inside, jnp.exp(-spot * spot / (2.0 * smooth_sigma * smooth_sigma)), 0.0) / normaliser

def thin_last(values):
    length = values.shape[-1]
    block_width = min(512, length)
    padded = jnp.pad(values, [(0, 0)] * (values.ndim - 1) + [(RADIUS, RADIUS)])
    row_ids = jnp.arange(block_width + 2 * RADIUS)[:, None]
    col_ids = jnp.arange(block_width // 4)[None, :]
    table = kernel(row_ids - RADIUS - 4 * col_ids)
    pieces = []
    for piece_num in range(length // block_width):
        window = padded[..., piece_num * block_width:piece_num * block_width + block_width + 2 * RADIUS]
        pieces.append(jnp.einsum('...p,pq->...q', window, table, precision=lax.Precision.HIGHEST))
    return jnp.concatenate(pieces, axis=-1)

def spread_last(values):
    coarse_len = values.shape[-1]
    block_width = min(512, 4 * coarse_len)
    margin = RADIUS // 4
    padded = jnp.pad(values, [(0, 0)] * (values.ndim - 1) + [(margin, margin)])
    row_ids = jnp.arange(block_width // 4 + 2 * margin)[:, None]
    col_ids = jnp.arange(block_width)[None, :]
    table = kernel(col_ids - 4 * (row_ids - margin))
    pieces = []
    for piece_num in range(4 * coarse_len // block_width):
        start = piece_num * block_width // 4
        window = padded[..., start:start + block_width // 4 + 2 * margin]
        pieces.append(jnp.einsum('...q,qp->...p', window, table, precision=lax.Precision.HIGHEST))
    return jnp.concatenate(pieces, axis=-1)

def soft_sign(diff):
    return diff * lax.rsqrt(diff * diff + huber_width * huber_width)

def reference(fields, observed):

    def smooth_member(member_field):
        lon_pass = thin_last(member_field)
        both = thin_last(jnp.swapaxes(lon_pass, 1, 2))
        return jnp.swapaxes(both, 1, 2)
    coarse = lax.map(smooth_member, fields)
    grad_scale = 64.0 * ENS

    def adjoint_member(member_rows):
        own_term = soft_sign(member_rows - observed) / ENS
        pair_term = lax.optimization_barrier(jnp.sum(soft_sign(member_rows[None] - coarse), axis=0))
        cell_grad = own_term - pair_term / (ENS * (ENS - 1))
        lat_back = spread_last(jnp.swapaxes(cell_grad, 1, 2))
        lon_back = spread_last(jnp.swapaxes(lat_back, 1, 2))
        return grad_scale * lon_back
    return lax.map(adjoint_member, coarse)
```

```python
import functools

import jax
import jax.numpy as jnp
import ml_dtypes
import numpy as np
from jax import lax
from jax.experimental import pallas as pl
from jax.experimental.pallas import tpu as pltpu
from jax.sharding import PartitionSpec as P

RADIUS = 16
SIGMA = 6.0
HUBER = 0.05
STRIDE = 4
MARGIN = RADIUS // STRIDE
LANES = 128
BLOCK = 256
VMEM = 48 * 1024 * 1024


def kern(offset):
    taps = np.arange(-RADIUS, RADIUS + 1).astype(np.float64)
    norm = np.sum(np.exp(-taps * taps / (2.0 * SIGMA * SIGMA)))
    spot = np.asarray(offset).astype(np.float64)
    inside = np.abs(spot) <= RADIUS
    return np.where(inside, np.exp(-spot * spot / (2.0 * SIGMA * SIGMA)), 0.0) / norm


def parts(table):
    high = table.astype(np.float32).astype(ml_dtypes.bfloat16)
    low = (table - high.astype(np.float64)).astype(ml_dtypes.bfloat16)
    return high, low


def lon_offsets():
    lane = np.arange(LANES)
    even = np.where(lane < LANES - MARGIN, lane, lane - LANES)
    odd = np.where(lane < MARGIN, lane + LANES, lane) - LANES // 2
    fine = np.arange(BLOCK)
    return [fine[:, None] - STRIDE * place[None, :] for place in (even, odd)]


def thin_lon_table():
    pairs = [parts(kern(offset)) for offset in lon_offsets()]
    return np.stack([np.concatenate(pair, axis=1) for pair in pairs])


def spread_lon_table():
    pairs = [parts(kern(offset).T) for offset in lon_offsets()]
    return np.stack([np.concatenate([part, part], axis=0) for pair in pairs for part in pair])


def lat_offsets(rows):
    near = np.arange(rows // STRIDE + 2 * MARGIN) - MARGIN
    return np.arange(rows)[:, None] - STRIDE * near[None, :]


def thin_lat_table(rows):
    high, low = parts(kern(lat_offsets(rows)).T)
    return np.concatenate(
        [np.concatenate([high, high], axis=1), np.concatenate([low, low], axis=1)], axis=0
    )


def spread_lat_table(rows, scale):
    high, low = parts(scale * kern(lat_offsets(rows)))
    return np.concatenate([high, high, low], axis=1)


def dot(a, b):
    return jnp.dot(a, b, preferred_element_type=jnp.float32)


def split(value):
    high = value.astype(jnp.bfloat16)
    low = (value - high.astype(jnp.float32)).astype(jnp.bfloat16)
    return high, low


def thin_kernel(bands, where_ref, x_ref, lon_ref, lat_ref, top_ref, mid_ref, low_ref):
    variables, rows, length = x_ref.shape[1:]
    value = x_ref[0].reshape(variables * rows, length)
    sums = []
    for k in range(length // BLOCK):
        high, low = split(value[:, k * BLOCK : (k + 1) * BLOCK])
        table = lon_ref[k % 2]
        both = dot(high, table) + dot(low, table)
        sums.append(both[:, :LANES] + both[:, LANES:])
    lane = lax.broadcasted_iota(jnp.int32, sums[0].shape, 1)
    zero = jnp.zeros_like(sums[0])
    columns = []
    for j in range(len(sums) // 2):
        after = sums[2 * j + 2] if 2 * j + 2 < len(sums) else zero
        before = sums[2 * j - 1] if j > 0 else zero
        columns.append(
            jnp.where(lane >= LANES - MARGIN, after, sums[2 * j])
            + jnp.where(lane < MARGIN, before, sums[2 * j + 1])
        )
    thin = jnp.concatenate(columns, axis=1)
    band = where_ref[0]
    for v in range(variables):
        high, low = split(thin[v * rows : (v + 1) * rows])
        both = dot(lat_ref[...], jnp.concatenate([high, low], axis=0))
        half = both.shape[0] // 2
        coarse = both[:half] + both[half:]
        row = lax.broadcasted_iota(jnp.int32, (8, coarse.shape[1]), 0)
        top_ref[0, v] = jnp.where((row < MARGIN) & (band == 0), 0.0, coarse[:8])
        mid_ref[0, v] = coarse[8:16]
        low_ref[0, v] = jnp.where((row >= MARGIN) & (band == bands - 1), 0.0, coarse[16:])


def thin(fields, where, bands):
    members, variables, rows, length = fields.shape
    lon = thin_lon_table()
    lat = thin_lat_table(rows)
    columns = length // STRIDE
    tile = jax.ShapeDtypeStruct((members, variables, 8, columns), jnp.float32)
    spec = pl.BlockSpec((1, variables, 8, columns), lambda m: (m, 0, 0, 0))
    return pl.pallas_call(
        functools.partial(thin_kernel, bands),
        grid=(members,),
        in_specs=[
            pl.BlockSpec(memory_space=pltpu.SMEM),
            pl.BlockSpec((1, variables, rows, length), lambda m: (m, 0, 0, 0)),
            pl.BlockSpec(lon.shape, lambda m: (0, 0, 0)),
            pl.BlockSpec(lat.shape, lambda m: (0, 0)),
        ],
        out_specs=[spec] * 3,
        out_shape=[tile] * 3,
        compiler_params=pltpu.CompilerParams(vmem_limit_bytes=VMEM),
        cost_estimate=pl.CostEstimate(flops=4_000_000_000, bytes_accessed=10_000_000, transcendentals=0),
    )(where, fields, jnp.asarray(lon), jnp.asarray(lat))


def soft_sign(diff):
    return diff * lax.rsqrt(diff * diff + HUBER * HUBER)


def pair_kernel(ensemble, own_ref, *refs):
    others, observed_ref, out_ref = refs[:-2], refs[-2], refs[-1]
    members = own_ref.shape[0]
    for j in range(own_ref.shape[-1] // LANES):
        columns = pl.ds(j * LANES, LANES)
        own = [own_ref[m, 0, :, columns] for m in range(members)]
        total = [None] * members
        for m in range(members):
            for n in range(m + 1, members):
                term = soft_sign(own[m] - own[n])
                total[m] = term if total[m] is None else total[m] + term
                total[n] = -term if total[n] is None else total[n] - term
        for other in others:
            for n in range(other.shape[0]):
                value = other[n, 0, :, columns]
                for m in range(members):
                    total[m] = total[m] + soft_sign(own[m] - value)
        seen = observed_ref[0, :, columns]
        for m in range(members):
            out_ref[m, 0, :, columns] = soft_sign(own[m] - seen) * (1.0 / ensemble) - total[m] * (
                1.0 / (ensemble * (ensemble - 1))
            )


def pair_gradient(own, others, observed, ensemble):
    members, variables, rows, columns = own.shape
    spec = pl.BlockSpec((members, 1, 8, columns), lambda v, r: (0, v, r, 0))
    return pl.pallas_call(
        functools.partial(pair_kernel, ensemble),
        grid=(variables, rows // 8),
        in_specs=[spec] * (1 + len(others))
        + [pl.BlockSpec((1, 8, columns), lambda v, r: (v, r, 0))],
        out_specs=spec,
        out_shape=jax.ShapeDtypeStruct(own.shape, jnp.float32),
        compiler_params=pltpu.CompilerParams(vmem_limit_bytes=VMEM),
        cost_estimate=pl.CostEstimate(flops=25_000_000, bytes_accessed=3_000_000, transcendentals=4_000_000),
    )(own, *others, observed)


def spread_kernel(bands, where_ref, top_ref, mid_ref, low_ref, lat_ref, lon_ref, out_ref):
    variables, rows, length = out_ref.shape[1:]
    band = where_ref[0]
    row = lax.broadcasted_iota(jnp.int32, top_ref.shape[2:], 0)
    tall = []
    for v in range(variables):
        top = jnp.where((row < MARGIN) & (band == 0), 0.0, top_ref[0, v])
        low = jnp.where((row >= MARGIN) & (band == bands - 1), 0.0, low_ref[0, v])
        grad = jnp.concatenate([top, mid_ref[0, v], low], axis=0)
        high = grad.astype(jnp.bfloat16).astype(jnp.float32)
        stack = jnp.concatenate([high, grad - high, high], axis=0).astype(jnp.bfloat16)
        tall.append(dot(lat_ref[...], stack))
    tall = jnp.concatenate(tall, axis=0)
    tiles = [tall[:, j * LANES : (j + 1) * LANES] for j in range(tall.shape[1] // LANES)]
    lane = lax.broadcasted_iota(jnp.int32, tiles[0].shape, 1)
    zero = jnp.zeros_like(tiles[0])
    for k in range(length // BLOCK):
        j = k // 2
        if k % 2 == 0:
            near = jnp.where(lane >= LANES - MARGIN, tiles[j - 1] if j > 0 else zero, tiles[j])
        else:
            near = jnp.where(lane < MARGIN, tiles[j + 1] if j + 1 < len(tiles) else zero, tiles[j])
        stack = jnp.concatenate(split(near), axis=1)
        wide = dot(stack, lon_ref[2 * (k % 2)]) + dot(stack, lon_ref[2 * (k % 2) + 1])
        out_ref[0, :, :, k * BLOCK : (k + 1) * BLOCK] = wide.reshape(variables, rows, BLOCK)


def spread(top, mid, low, where, bands, rows, length, scale):
    members, variables, _, columns = mid.shape
    lat = spread_lat_table(rows, scale)
    lon = spread_lon_table()
    spec = pl.BlockSpec((1, variables, 8, columns), lambda m: (m, 0, 0, 0))
    return pl.pallas_call(
        functools.partial(spread_kernel, bands),
        grid=(members,),
        in_specs=[
            pl.BlockSpec(memory_space=pltpu.SMEM),
            spec,
            spec,
            spec,
            pl.BlockSpec(lat.shape, lambda m: (0, 0)),
            pl.BlockSpec(lon.shape, lambda m: (0, 0, 0)),
        ],
        out_specs=pl.BlockSpec((1, variables, rows, length), lambda m: (m, 0, 0, 0)),
        out_shape=jax.ShapeDtypeStruct((members, variables, rows, length), jnp.float32),
        compiler_params=pltpu.CompilerParams(vmem_limit_bytes=VMEM),
        cost_estimate=pl.CostEstimate(flops=4_000_000_000, bytes_accessed=10_000_000, transcendentals=0),
    )(where, top, mid, low, jnp.asarray(lat), jnp.asarray(lon))


def swap(value, bit):
    devices = lax.axis_size("member")
    return lax.ppermute(value, "member", [(i, i ^ bit) for i in range(devices)])


def shards(fields, observed):
    members, _, rows, length = fields.shape
    bands = lax.axis_size("band")
    ensemble = members * lax.axis_size("member")
    where = lax.axis_index("band").astype(jnp.int32).reshape(1)
    up = [(i, (i + 1) % bands) for i in range(bands)]
    down = [(j, i) for i, j in up]
    seen = lax.ppermute(observed[:, -MARGIN:], "band", up)
    seen = jnp.concatenate([seen, observed[:, :-MARGIN]], axis=1)
    top, mid, low = thin(fields, where, bands)
    top = top + lax.ppermute(low, "band", up)
    own = jnp.concatenate([top, mid], axis=2)
    beside = swap(own, 1)
    across = swap(own, 2)
    corner = swap(across, 1)
    grad = pair_gradient(own, [beside, across, corner], seen, ensemble)
    top, mid = grad[:, :, :8], grad[:, :, 8:]
    low = lax.ppermute(top, "band", down)
    return spread(top, mid, low, where, bands, rows, length, 64.0 * ensemble)


def solution(mesh):
    return jax.shard_map(
        shards,
        mesh=mesh,
        in_specs=(P("member", None, "band", None), P(None, "band", None)),
        out_specs=P("member", None, "band", None),
        check_vma=False,
    )
```

```python
import functools

import jax
import jax.numpy as jnp
import ml_dtypes
import numpy as np
from jax import lax
from jax.experimental import pallas as pl
from jax.experimental.pallas import tpu as pltpu
from jax.sharding import PartitionSpec as P

RADIUS = 16
SIGMA = 6.0
HUBER = 0.05
STRIDE = 4
MARGIN = RADIUS // STRIDE
LANES = 128
BLOCK = 256
TILE = 8
HALF = 32
NEAR = HALF // STRIDE + 2 * MARGIN
GROUP = 2
AHEAD = 3
VMEM = 40 * 1024 * 1024
WHOLE = 50 * 1024 * 1024


def kern(offset):
    taps = np.arange(-RADIUS, RADIUS + 1).astype(np.float64)
    norm = np.sum(np.exp(-taps * taps / (2.0 * SIGMA * SIGMA)))
    spot = np.asarray(offset).astype(np.float64)
    inside = np.abs(spot) <= RADIUS
    return np.where(inside, np.exp(-spot * spot / (2.0 * SIGMA * SIGMA)), 0.0) / norm


def parts(table):
    high = table.astype(np.float32).astype(ml_dtypes.bfloat16)
    low = (table - high.astype(np.float64)).astype(ml_dtypes.bfloat16)
    return high, low


def lon_offsets():
    lane = np.arange(LANES)
    even = np.where(lane < LANES - MARGIN, lane, lane - LANES)
    odd = np.where(lane < MARGIN, lane + LANES, lane) - LANES // 2
    fine = np.arange(BLOCK)
    return [fine[:, None] - STRIDE * place[None, :] for place in (even, odd)]


def spread_lon_table():
    pairs = [parts(kern(offset).T) for offset in lon_offsets()]
    return np.stack([np.concatenate([part, part], axis=0) for pair in pairs for part in pair])


def half_table():
    near = np.arange(NEAR) - MARGIN
    return kern(np.arange(HALF)[:, None] - STRIDE * near[None, :])


def per_image(table, images):
    eye = np.eye(images, dtype=np.float32)
    return np.kron(eye, table.astype(np.float32)).astype(ml_dtypes.bfloat16)


def spread_lat_table(images, scale):
    high, low = (per_image(part, images) for part in parts(scale * half_table()))
    return np.concatenate([high, high, low], axis=1)


def dot(a, b):
    return jnp.dot(a, b, preferred_element_type=jnp.float32)


def split(value):
    high = value.astype(jnp.bfloat16)
    low = (value - high.astype(jnp.float32)).astype(jnp.bfloat16)
    return high, low


def outside(shape, axis, band, bands, half):
    row = lax.broadcasted_iota(jnp.int32, shape, axis)
    above = (row < MARGIN) & (band == 0) & (half == 0)
    below = (row >= MARGIN) & (band == bands - 1) & (half == 1)
    return above | below


def taps(offset):
    norm = np.sum(np.exp(-np.arange(-RADIUS, RADIUS + 1).astype(np.float64) ** 2 / (2.0 * SIGMA * SIGMA)))
    spot = offset.astype(jnp.float32)
    value = jnp.exp(spot * spot * (-1.0 / (2.0 * SIGMA * SIGMA))) * (1.0 / norm)
    return jnp.where(jnp.abs(offset) <= RADIUS, value, 0.0)


def fill_thin_tables(lon_ref, lat_ref, variables, rows):
    shape = (BLOCK, LANES)
    fine = lax.broadcasted_iota(jnp.int32, shape, 0)
    lane = lax.broadcasted_iota(jnp.int32, shape, 1)
    even = jnp.where(lane < LANES - MARGIN, lane, lane - LANES)
    odd = jnp.where(lane < MARGIN, lane + LANES, lane) - LANES // 2
    for i, place in enumerate((even, odd)):
        high, low = split(taps(fine - STRIDE * place))
        lon_ref[i, :, :LANES] = high
        lon_ref[i, :, LANES:] = low
    near = rows // STRIDE + 2 * MARGIN
    depth = variables * rows
    shape = (variables * near, depth)
    out = lax.broadcasted_iota(jnp.int32, shape, 0)
    row = lax.broadcasted_iota(jnp.int32, shape, 1)
    image = sum((out >= v * near).astype(jnp.int32) for v in range(1, variables))
    offset = (row - image * rows) - STRIDE * (out - image * near - MARGIN)
    inside = (row >= image * rows) & (row < (image + 1) * rows)
    high, low = split(jnp.where(inside, taps(offset), 0.0))
    for part, value in enumerate((high, low)):
        place = pl.ds(part * variables * near, variables * near)
        lat_ref[place, :depth] = value
        lat_ref[place, depth:] = value


def thin_rows(value, lon_ref, lat_ref):
    variables, rows, length = value.shape
    value = value.reshape(variables * rows, length)
    count = length // BLOCK
    depth = value.shape[0]
    half = count // 2
    sums = [None] * count
    for odd in range(2):
        pairs = [split(value[:, k * BLOCK : (k + 1) * BLOCK]) for k in range(odd, count, 2)]
        stack = jnp.concatenate([p[0] for p in pairs] + [p[1] for p in pairs], axis=0)
        both = dot(stack, lon_ref[odd])
        both = both[:, :LANES] + both[:, LANES:]
        for i in range(half):
            sums[2 * i + odd] = (
                both[i * depth : (i + 1) * depth]
                + both[(half + i) * depth : (half + i + 1) * depth]
            )
    lane = lax.broadcasted_iota(jnp.int32, sums[0].shape, 1)
    zero = jnp.zeros_like(sums[0])
    columns = []
    for j in range(half):
        after = sums[2 * j + 2] if 2 * j + 2 < count else zero
        before = sums[2 * j - 1] if j > 0 else zero
        columns.append(
            jnp.where(lane >= LANES - MARGIN, after, sums[2 * j])
            + jnp.where(lane < MARGIN, before, sums[2 * j + 1])
        )
    high, low = split(jnp.concatenate(columns, axis=1))
    both = dot(lat_ref[...], jnp.concatenate([high, low], axis=0))
    middle = both.shape[0] // 2
    coarse = both[:middle] + both[middle:]
    return coarse.reshape(variables, 3, TILE, length // STRIDE)


def thin_kernel(bands, where_ref, x_ref, seen_hbm, near_ref, far_ref, mid_ref, held, lon_ref, lat_ref, seen_ref, arrived, seen_here):
    band = where_ref[0]
    even = band % 2 == 0
    members, variables, rows, _ = held.shape

    def copy(m):
        return pltpu.make_async_copy(x_ref.at[m], held.at[m], arrived.at[m])

    for m in range(AHEAD):
        copy(m).start()
    seen_copy = pltpu.make_async_copy(seen_hbm, seen_ref, seen_here)
    seen_copy.start()
    fill_thin_tables(lon_ref, lat_ref, variables, rows)
    for m in range(members):
        copy(m).wait()
        if m + AHEAD < members:
            copy(m + AHEAD).start()
        coarse = thin_rows(held[m], lon_ref, lat_ref)
        upper, lower = coarse[:, 0], coarse[:, 2]
        upper = jnp.where(outside(upper.shape, 1, band, bands, 0), 0.0, upper)
        lower = jnp.where(outside(lower.shape, 1, band, bands, 1), 0.0, lower)
        near_ref[m] = jnp.where(even, lower, upper)
        far_ref[m] = jnp.where(even, upper, lower)
        mid_ref[m] = coarse[:, 1]
    seen_copy.wait()
    seen = seen_ref[...]
    zero = jnp.zeros((seen.shape[0], MARGIN, seen.shape[2]), jnp.float32)
    upper = jnp.concatenate([zero, seen[:, :MARGIN]], axis=1)
    lower = jnp.concatenate([seen[:, -MARGIN:], zero], axis=1)
    near_ref[members] = jnp.where(even, lower, upper)
    far_ref[members] = jnp.where(even, upper, lower)


def thin(fields, observed, where, bands):
    members, variables, rows, length = fields.shape
    columns = length // STRIDE
    near = rows // STRIDE + 2 * MARGIN
    full = pl.BlockSpec(memory_space=pltpu.VMEM)
    any_space = pl.BlockSpec(memory_space=pl.ANY)
    edge = jax.ShapeDtypeStruct((members + 1, variables, TILE, columns), jnp.float32)
    return pl.pallas_call(
        functools.partial(thin_kernel, bands),
        in_specs=[pl.BlockSpec(memory_space=pltpu.SMEM), any_space, any_space],
        out_specs=[full] * 3,
        out_shape=[edge, edge, jax.ShapeDtypeStruct((members, variables, TILE, columns), jnp.float32)],
        scratch_shapes=[
            pltpu.VMEM(fields.shape, jnp.float32),
            pltpu.VMEM((2, BLOCK, 2 * LANES), jnp.bfloat16),
            pltpu.VMEM((2 * variables * near, 2 * variables * rows), jnp.bfloat16),
            pltpu.VMEM(observed.shape, jnp.float32),
            pltpu.SemaphoreType.DMA((members,)),
            pltpu.SemaphoreType.DMA,
        ],
        compiler_params=pltpu.CompilerParams(vmem_limit_bytes=WHOLE),
        cost_estimate=pl.CostEstimate(flops=1, bytes_accessed=1, transcendentals=0),
    )(where, fields, observed)


def soft_sign(diff):
    return diff * lax.rsqrt(diff * diff + HUBER * HUBER)


def pair_kernel(ensemble, own_ref, beside_ref, across_ref, corner_ref, seen_ref, out_ref):
    members, variables, _, columns = own_ref.shape
    tiles = columns // LANES

    def step(i, carry):
        v = i // tiles
        place = pl.ds(pl.multiple_of((i % tiles) * LANES, LANES), LANES)
        own = [own_ref[m, v, :, place] for m in range(members)]
        total = [None] * members
        for m in range(members):
            for n in range(m + 1, members):
                term = soft_sign(own[m] - own[n])
                total[m] = term if total[m] is None else total[m] + term
                total[n] = -term if total[n] is None else total[n] - term
        for other in (beside_ref, across_ref, corner_ref):
            for n in range(members):
                value = other[n, v, :, place]
                for m in range(members):
                    total[m] = total[m] + soft_sign(own[m] - value)
        seen = seen_ref[v, :, place]
        for m in range(members):
            out_ref[m, v, :, place] = soft_sign(own[m] - seen) * (1.0 / ensemble) - total[m] * (
                1.0 / (ensemble * (ensemble - 1))
            )
        return carry

    lax.fori_loop(0, variables * tiles, step, 0)


def pair_gradient(own, beside, across, corner, seen, ensemble):
    full = pl.BlockSpec(memory_space=pltpu.VMEM)
    return pl.pallas_call(
        functools.partial(pair_kernel, ensemble),
        in_specs=[full] * 5,
        out_specs=full,
        out_shape=jax.ShapeDtypeStruct(own.shape, jnp.float32),
        compiler_params=pltpu.CompilerParams(vmem_limit_bytes=VMEM),
        cost_estimate=pl.CostEstimate(flops=1, bytes_accessed=1, transcendentals=0),
    )(own, beside, across, corner, seen)


def spread_rows(edge, mid, band, bands, half, lat_ref, lon_ref, store):
    group, variables, _, columns = edge.shape
    edge = jnp.where(outside(edge.shape, 2, band, bands, half), 0.0, edge)
    upper = jnp.where(half == 0, edge, mid)
    lower = jnp.where(half == 0, mid, edge)
    grad = jnp.stack([upper, lower], axis=2).reshape(group * variables * NEAR, columns)
    high, low = split(grad)
    tall = dot(lat_ref[...], jnp.concatenate([high, low, high], axis=0))
    depth = tall.shape[0]
    tiles = [tall[:, j * LANES : (j + 1) * LANES] for j in range(columns // LANES)]
    lane = lax.broadcasted_iota(jnp.int32, tiles[0].shape, 1)
    zero = jnp.zeros_like(tiles[0])
    count = len(tiles)
    for odd in range(2):
        stacks = []
        for j in range(count):
            if odd:
                after = tiles[j + 1] if j + 1 < count else zero
                near = jnp.where(lane < MARGIN, after, tiles[j])
            else:
                before = tiles[j - 1] if j > 0 else zero
                near = jnp.where(lane >= LANES - MARGIN, before, tiles[j])
            stacks.append(jnp.concatenate(split(near), axis=1))
        stack = jnp.concatenate(stacks, axis=0)
        wide = dot(stack, lon_ref[2 * odd]) + dot(stack, lon_ref[2 * odd + 1])
        for j in range(count):
            store(2 * j + odd, wide[j * depth : (j + 1) * depth].reshape(group, variables, HALF, BLOCK))


def spread_kernel(bands, where_ref, *refs):
    edge_ref, mid_ref, lat_ref, lon_ref, out_ref, held, sent = refs[-7:]
    band, half = where_ref[0], where_ref[1]
    members = held.shape[0]
    start = pl.multiple_of(half * HALF, HALF)

    def copy(c):
        group = pl.ds(c * GROUP, GROUP)
        return pltpu.make_async_copy(
            held.at[group], out_ref.at[group, :, pl.ds(start, HALF), :], sent.at[c]
        )

    chunks = members // GROUP
    for c in range(chunks):
        group = pl.ds(c * GROUP, GROUP)

        def store(k, value, group=group):
            held[group, :, :, k * BLOCK : (k + 1) * BLOCK] = value

        spread_rows(edge_ref[group], mid_ref[group], band, bands, half, lat_ref, lon_ref, store)
        copy(c).start()
    for c in range(chunks):
        copy(c).wait()


def spread(edge, mid, where, bands, shape, scale, out=None):
    members, variables, _, length = shape
    lat = spread_lat_table(GROUP * variables, scale)
    lon = spread_lon_table()
    full = pl.BlockSpec(memory_space=pltpu.VMEM)
    any_space = pl.BlockSpec(memory_space=pl.ANY)
    extra = [] if out is None else [out]
    return pl.pallas_call(
        functools.partial(spread_kernel, bands),
        in_specs=[pl.BlockSpec(memory_space=pltpu.SMEM)] + [any_space] * len(extra) + [full] * 4,
        out_specs=any_space,
        out_shape=jax.ShapeDtypeStruct(shape, jnp.float32),
        scratch_shapes=[
            pltpu.VMEM((members, variables, HALF, length), jnp.float32),
            pltpu.SemaphoreType.DMA((members // GROUP,)),
        ],
        input_output_aliases={1: 0} if extra else {},
        compiler_params=pltpu.CompilerParams(vmem_limit_bytes=VMEM),
        cost_estimate=pl.CostEstimate(flops=1, bytes_accessed=1, transcendentals=0),
    )(where, *extra, edge, mid, jnp.asarray(lat), jnp.asarray(lon))


def swap(value, bit):
    devices = lax.axis_size("member")
    return lax.ppermute(value, "member", [(i, i ^ bit) for i in range(devices)])


def pairs_of(bands, first):
    pairs = [(i, i + 1) for i in range(first, bands - 1, 2)]
    return pairs + [(j, i) for i, j in pairs]


def shards(fields, observed):
    members, _, rows, _ = fields.shape
    bands = lax.axis_size("band")
    ensemble = members * lax.axis_size("member")
    band = lax.axis_index("band").astype(jnp.int32)
    far = jnp.stack([band, band % 2])
    near = jnp.stack([band, 1 - band % 2])
    tie = lax.optimization_barrier
    near_part, far_part, mid = thin(fields, observed, band.reshape(1), bands)
    far_come = lax.ppermute(far_part, "band", pairs_of(bands, 1))
    near_come = lax.ppermute(near_part, "band", pairs_of(bands, 0))
    across_mid = swap(mid, 2)
    beside_mid = swap(mid, 1)
    near_tile = near_part[:members] + near_come[:members]
    near_seen = near_part[members] + near_come[members]
    across_near = swap(near_tile, 2)
    beside_near = swap(near_tile, 1)
    across_mid, near_tile = tie((across_mid, near_tile))
    corner_mid = swap(across_mid, 1)
    seen = observed[:, MARGIN:-MARGIN]
    mid_grad = pair_gradient(mid, beside_mid, across_mid, corner_mid, seen, ensemble)
    far_come, mid_grad = tie((far_come, mid_grad))
    far_tile = far_part[:members] + far_come[:members]
    far_seen = far_part[members] + far_come[members]
    across_far = swap(far_tile, 2)
    beside_far = swap(far_tile, 1)
    across_near, beside_far = tie((across_near, beside_far))
    corner_near = swap(across_near, 1)
    near_grad = pair_gradient(near_tile, beside_near, across_near, corner_near, near_seen, ensemble)
    scale = 64.0 * ensemble
    out = spread(near_grad, mid_grad, near, bands, fields.shape, scale)
    across_far, out = tie((across_far, out))
    corner_far = swap(across_far, 1)
    far_grad = pair_gradient(far_tile, beside_far, across_far, corner_far, far_seen, ensemble)
    return spread(far_grad, mid_grad, far, bands, fields.shape, scale, out)


def solution(mesh):
    return jax.shard_map(
        shards,
        mesh=mesh,
        in_specs=(P("member", None, "band", None), P(None, "band", None)),
        out_specs=P("member", None, "band", None),
        check_vma=False,
    )
```

```python
import functools

import jax
import jax.numpy as jnp
import ml_dtypes
import numpy as np
from jax import lax
from jax.experimental import pallas as pl
from jax.experimental.pallas import tpu as pltpu
from jax.sharding import PartitionSpec as P

RADIUS = 16
SIGMA = 6.0
HUBER = 0.05
STRIDE = 4
MARGIN = RADIUS // STRIDE
LANES = 128
BLOCK = 256
TILE = 8
HALF = 32
NEAR = HALF // STRIDE + 2 * MARGIN
GROUP = 2
AHEAD = 3
VMEM = 40 * 1024 * 1024
WHOLE = 50 * 1024 * 1024


def kern(offset):
    taps = np.arange(-RADIUS, RADIUS + 1).astype(np.float64)
    norm = np.sum(np.exp(-taps * taps / (2.0 * SIGMA * SIGMA)))
    spot = np.asarray(offset).astype(np.float64)
    inside = np.abs(spot) <= RADIUS
    return np.where(inside, np.exp(-spot * spot / (2.0 * SIGMA * SIGMA)), 0.0) / norm


def parts(table):
    high = table.astype(np.float32).astype(ml_dtypes.bfloat16)
    low = (table - high.astype(np.float64)).astype(ml_dtypes.bfloat16)
    return high, low


def lon_offsets():
    lane = np.arange(LANES)
    even = np.where(lane < LANES - MARGIN, lane, lane - LANES)
    odd = np.where(lane < MARGIN, lane + LANES, lane) - LANES // 2
    fine = np.arange(BLOCK)
    return [fine[:, None] - STRIDE * place[None, :] for place in (even, odd)]


def spread_lon_table():
    pairs = [parts(kern(offset).T) for offset in lon_offsets()]
    return np.stack([np.concatenate([part, part], axis=0) for pair in pairs for part in pair])


def half_table():
    near = np.arange(NEAR) - MARGIN
    return kern(np.arange(HALF)[:, None] - STRIDE * near[None, :])


def per_image(table, images):
    eye = np.eye(images, dtype=np.float32)
    return np.kron(eye, table.astype(np.float32)).astype(ml_dtypes.bfloat16)


def spread_lat_table(images, scale):
    high, low = (per_image(part, images) for part in parts(scale * half_table()))
    return np.concatenate([high, high, low], axis=1)


def dot(a, b):
    return jnp.dot(a, b, preferred_element_type=jnp.float32)


def split(value):
    high = value.astype(jnp.bfloat16)
    low = (value - high.astype(jnp.float32)).astype(jnp.bfloat16)
    return high, low


def outside(shape, axis, band, bands, half):
    row = lax.broadcasted_iota(jnp.int32, shape, axis)
    above = (row < MARGIN) & (band == 0) & (half == 0)
    below = (row >= MARGIN) & (band == bands - 1) & (half == 1)
    return above | below


def taps(offset):
    norm = np.sum(np.exp(-np.arange(-RADIUS, RADIUS + 1).astype(np.float64) ** 2 / (2.0 * SIGMA * SIGMA)))
    spot = offset.astype(jnp.float32)
    value = jnp.exp(spot * spot * (-1.0 / (2.0 * SIGMA * SIGMA))) * (1.0 / norm)
    return jnp.where(jnp.abs(offset) <= RADIUS, value, 0.0)


def fill_thin_tables(lon_ref, lat_ref, variables, rows):
    shape = (BLOCK, LANES)
    fine = lax.broadcasted_iota(jnp.int32, shape, 0)
    lane = lax.broadcasted_iota(jnp.int32, shape, 1)
    even = jnp.where(lane < LANES - MARGIN, lane, lane - LANES)
    odd = jnp.where(lane < MARGIN, lane + LANES, lane) - LANES // 2
    for i, place in enumerate((even, odd)):
        high, low = split(taps(fine - STRIDE * place))
        lon_ref[i, :, :LANES] = high
        lon_ref[i, :, LANES:] = low
    near = rows // STRIDE + 2 * MARGIN
    depth = variables * rows
    shape = (variables * near, depth)
    out = lax.broadcasted_iota(jnp.int32, shape, 0)
    row = lax.broadcasted_iota(jnp.int32, shape, 1)
    image = sum((out >= v * near).astype(jnp.int32) for v in range(1, variables))
    offset = (row - image * rows) - STRIDE * (out - image * near - MARGIN)
    inside = (row >= image * rows) & (row < (image + 1) * rows)
    high, low = split(jnp.where(inside, taps(offset), 0.0))
    for part, value in enumerate((high, low)):
        place = pl.ds(part * variables * near, variables * near)
        lat_ref[place, :depth] = value
        lat_ref[place, depth:] = value


def thin_rows(value, lon_ref, lat_ref):
    variables, rows, length = value.shape
    value = value.reshape(variables * rows, length)
    count = length // BLOCK
    depth = value.shape[0]
    half = count // 2
    sums = [None] * count
    for odd in range(2):
        pairs = [split(value[:, k * BLOCK : (k + 1) * BLOCK]) for k in range(odd, count, 2)]
        stack = jnp.concatenate([p[0] for p in pairs] + [p[1] for p in pairs], axis=0)
        both = dot(stack, lon_ref[odd])
        both = both[:, :LANES] + both[:, LANES:]
        for i in range(half):
            sums[2 * i + odd] = (
                both[i * depth : (i + 1) * depth]
                + both[(half + i) * depth : (half + i + 1) * depth]
            )
    lane = lax.broadcasted_iota(jnp.int32, sums[0].shape, 1)
    zero = jnp.zeros_like(sums[0])
    columns = []
    for j in range(half):
        after = sums[2 * j + 2] if 2 * j + 2 < count else zero
        before = sums[2 * j - 1] if j > 0 else zero
        columns.append(
            jnp.where(lane >= LANES - MARGIN, after, sums[2 * j])
            + jnp.where(lane < MARGIN, before, sums[2 * j + 1])
        )
    high, low = split(jnp.concatenate(columns, axis=1))
    both = dot(lat_ref[...], jnp.concatenate([high, low], axis=0))
    middle = both.shape[0] // 2
    coarse = both[:middle] + both[middle:]
    return coarse.reshape(variables, 3, TILE, length // STRIDE)


def thin_kernel(bands, where_ref, x_ref, seen_hbm, near_ref, far_ref, mid_ref, held, lon_ref, lat_ref, seen_ref, arrived, seen_here):
    band = where_ref[0]
    even = band % 2 == 0
    members, variables, rows, _ = held.shape

    def copy(m):
        return pltpu.make_async_copy(x_ref.at[m], held.at[m], arrived.at[m])

    for m in range(AHEAD):
        copy(m).start()
    seen_copy = pltpu.make_async_copy(seen_hbm, seen_ref, seen_here)
    seen_copy.start()
    fill_thin_tables(lon_ref, lat_ref, variables, rows)
    for m in range(members):
        copy(m).wait()
        if m + AHEAD < members:
            copy(m + AHEAD).start()
        coarse = thin_rows(held[m], lon_ref, lat_ref)
        upper, lower = coarse[:, 0], coarse[:, 2]
        upper = jnp.where(outside(upper.shape, 1, band, bands, 0), 0.0, upper)
        lower = jnp.where(outside(lower.shape, 1, band, bands, 1), 0.0, lower)
        near_ref[m] = jnp.where(even, lower, upper)
        far_ref[m] = jnp.where(even, upper, lower)
        mid_ref[m] = coarse[:, 1]
    seen_copy.wait()
    seen = seen_ref[...]
    zero = jnp.zeros((seen.shape[0], MARGIN, seen.shape[2]), jnp.float32)
    upper = jnp.concatenate([zero, seen[:, :MARGIN]], axis=1)
    lower = jnp.concatenate([seen[:, -MARGIN:], zero], axis=1)
    near_ref[members] = jnp.where(even, lower, upper)
    far_ref[members] = jnp.where(even, upper, lower)


def thin(fields, observed, where, bands):
    members, variables, rows, length = fields.shape
    columns = length // STRIDE
    near = rows // STRIDE + 2 * MARGIN
    full = pl.BlockSpec(memory_space=pltpu.VMEM)
    any_space = pl.BlockSpec(memory_space=pl.ANY)
    edge = jax.ShapeDtypeStruct((members + 1, variables, TILE, columns), jnp.float32)
    return pl.pallas_call(
        functools.partial(thin_kernel, bands),
        in_specs=[pl.BlockSpec(memory_space=pltpu.SMEM), any_space, any_space],
        out_specs=[full] * 3,
        out_shape=[edge, edge, jax.ShapeDtypeStruct((members, variables, TILE, columns), jnp.float32)],
        scratch_shapes=[
            pltpu.VMEM(fields.shape, jnp.float32),
            pltpu.VMEM((2, BLOCK, 2 * LANES), jnp.bfloat16),
            pltpu.VMEM((2 * variables * near, 2 * variables * rows), jnp.bfloat16),
            pltpu.VMEM(observed.shape, jnp.float32),
            pltpu.SemaphoreType.DMA((members,)),
            pltpu.SemaphoreType.DMA,
        ],
        compiler_params=pltpu.CompilerParams(vmem_limit_bytes=WHOLE),
        cost_estimate=pl.CostEstimate(flops=1, bytes_accessed=1, transcendentals=0),
    )(where, fields, observed)


def soft_sign(diff):
    return diff * lax.rsqrt(diff * diff + HUBER * HUBER)


def pair_kernel(ensemble, own_ref, beside_ref, across_ref, seen_ref, out_ref):
    members, variables, _, columns = own_ref.shape
    tiles = columns // LANES

    def step(i, carry):
        v = i // tiles
        place = pl.ds(pl.multiple_of((i % tiles) * LANES, LANES), LANES)
        own = [own_ref[m, v, :, place] for m in range(members)]
        total = [None] * members
        for m in range(members):
            for n in range(m + 1, members):
                term = soft_sign(own[m] - own[n])
                total[m] = term if total[m] is None else total[m] + term
                total[n] = -term if total[n] is None else total[n] - term
        for other in (beside_ref, across_ref):
            for n in range(members):
                value = other[n, v, :, place]
                for m in range(members):
                    total[m] = total[m] + soft_sign(own[m] - value)
        seen = seen_ref[v, :, place]
        for m in range(members):
            out_ref[m, v, :, place] = soft_sign(own[m] - seen) * (1.0 / ensemble) - total[m] * (
                1.0 / (ensemble * (ensemble - 1))
            )
        return carry

    lax.fori_loop(0, variables * tiles, step, 0)


def pair_gradient(own, beside, across, seen, ensemble):
    full = pl.BlockSpec(memory_space=pltpu.VMEM)
    return pl.pallas_call(
        functools.partial(pair_kernel, ensemble),
        in_specs=[full] * 4,
        out_specs=full,
        out_shape=jax.ShapeDtypeStruct(own.shape, jnp.float32),
        compiler_params=pltpu.CompilerParams(vmem_limit_bytes=VMEM),
        cost_estimate=pl.CostEstimate(flops=1, bytes_accessed=1, transcendentals=0),
    )(own, beside, across, seen)


def finish(ensemble, group, own_ref, part_ref, corner_ref):
    own = own_ref[group]
    total = jnp.zeros_like(own)
    for n in range(corner_ref.shape[0]):
        total = total + soft_sign(own - corner_ref[n][None])
    return part_ref[group] - total * (1.0 / (ensemble * (ensemble - 1)))


def spread_rows(edge, mid, band, bands, half, lat_ref, lon_ref, store):
    group, variables, _, columns = edge.shape
    edge = jnp.where(outside(edge.shape, 2, band, bands, half), 0.0, edge)
    upper = jnp.where(half == 0, edge, mid)
    lower = jnp.where(half == 0, mid, edge)
    grad = jnp.stack([upper, lower], axis=2).reshape(group * variables * NEAR, columns)
    high, low = split(grad)
    tall = dot(lat_ref[...], jnp.concatenate([high, low, high], axis=0))
    depth = tall.shape[0]
    tiles = [tall[:, j * LANES : (j + 1) * LANES] for j in range(columns // LANES)]
    lane = lax.broadcasted_iota(jnp.int32, tiles[0].shape, 1)
    zero = jnp.zeros_like(tiles[0])
    count = len(tiles)
    for odd in range(2):
        stacks = []
        for j in range(count):
            if odd:
                after = tiles[j + 1] if j + 1 < count else zero
                near = jnp.where(lane < MARGIN, after, tiles[j])
            else:
                before = tiles[j - 1] if j > 0 else zero
                near = jnp.where(lane >= LANES - MARGIN, before, tiles[j])
            stacks.append(jnp.concatenate(split(near), axis=1))
        stack = jnp.concatenate(stacks, axis=0)
        wide = dot(stack, lon_ref[2 * odd]) + dot(stack, lon_ref[2 * odd + 1])
        for j in range(count):
            store(2 * j + odd, wide[j * depth : (j + 1) * depth].reshape(group, variables, HALF, BLOCK))


def spread_kernel(bands, ensemble, first, where_ref, *refs):
    if first:
        edge_trio, mid_trio = refs[:3], refs[3:6]
        lat_ref, lon_ref, out_ref, mid_ref, held, sent = refs[6:]
    else:
        edge_trio, mid_ref = refs[1:4], refs[4]
        lat_ref, lon_ref, out_ref, held, sent = refs[5:]
    band, half = where_ref[0], where_ref[1]
    members = held.shape[0]
    start = pl.multiple_of(half * HALF, HALF)

    def copy(c):
        group = pl.ds(c * GROUP, GROUP)
        return pltpu.make_async_copy(
            held.at[group], out_ref.at[group, :, pl.ds(start, HALF), :], sent.at[c]
        )

    chunks = members // GROUP
    for c in range(chunks):
        group = pl.ds(c * GROUP, GROUP)

        def store(k, value, group=group):
            held[group, :, :, k * BLOCK : (k + 1) * BLOCK] = value

        edge = finish(ensemble, group, *edge_trio)
        if first:
            mid = finish(ensemble, group, *mid_trio)
            mid_ref[group] = mid
        else:
            mid = mid_ref[group]
        spread_rows(edge, mid, band, bands, half, lat_ref, lon_ref, store)
        copy(c).start()
    for c in range(chunks):
        copy(c).wait()


def spread(edge, mid, where, bands, shape, ensemble, out=None):
    members, variables, _, length = shape
    lat = spread_lat_table(GROUP * variables, 64.0 * ensemble)
    lon = spread_lon_table()
    tile = jax.ShapeDtypeStruct(edge[0].shape, jnp.float32)
    whole = jax.ShapeDtypeStruct(shape, jnp.float32)
    full = pl.BlockSpec(memory_space=pltpu.VMEM)
    any_space = pl.BlockSpec(memory_space=pl.ANY)
    first = out is None
    operands = [*edge, *mid] if first else [out, *edge, mid]
    return pl.pallas_call(
        functools.partial(spread_kernel, bands, ensemble, first),
        in_specs=[pl.BlockSpec(memory_space=pltpu.SMEM)]
        + ([full] * 6 if first else [any_space] + [full] * 4)
        + [full] * 2,
        out_specs=[any_space, full] if first else any_space,
        out_shape=[whole, tile] if first else whole,
        scratch_shapes=[
            pltpu.VMEM((members, variables, HALF, length), jnp.float32),
            pltpu.SemaphoreType.DMA((members // GROUP,)),
        ],
        input_output_aliases={} if first else {1: 0},
        compiler_params=pltpu.CompilerParams(vmem_limit_bytes=VMEM),
        cost_estimate=pl.CostEstimate(flops=1, bytes_accessed=1, transcendentals=0),
    )(where, *operands, jnp.asarray(lat), jnp.asarray(lon))


def swap(value, bit):
    devices = lax.axis_size("member")
    return lax.ppermute(value, "member", [(i, i ^ bit) for i in range(devices)])


def pairs_of(bands, first):
    pairs = [(i, i + 1) for i in range(first, bands - 1, 2)]
    return pairs + [(j, i) for i, j in pairs]


def shards(fields, observed):
    members, _, rows, _ = fields.shape
    bands = lax.axis_size("band")
    ensemble = members * lax.axis_size("member")
    band = lax.axis_index("band").astype(jnp.int32)
    far = jnp.stack([band, band % 2])
    near = jnp.stack([band, 1 - band % 2])
    tie = lax.optimization_barrier
    near_part, far_part, mid = thin(fields, observed, band.reshape(1), bands)
    far_come = lax.ppermute(far_part, "band", pairs_of(bands, 1))
    near_come = lax.ppermute(near_part, "band", pairs_of(bands, 0))
    across_mid = swap(mid, 2)
    beside_mid = swap(mid, 1)
    near_tile = near_part[:members] + near_come[:members]
    near_seen = near_part[members] + near_come[members]
    across_near = swap(near_tile, 2)
    beside_near = swap(near_tile, 1)
    across_mid, near_tile = tie((across_mid, near_tile))
    corner_mid = swap(across_mid, 1)
    beside_mid, corner_mid = tie((beside_mid, corner_mid))
    mid_part = pair_gradient(mid, beside_mid, across_mid, observed[:, MARGIN:-MARGIN], ensemble)
    far_come, mid_part = tie((far_come, mid_part))
    far_tile = far_part[:members] + far_come[:members]
    far_seen = far_part[members] + far_come[members]
    across_far = swap(far_tile, 2)
    beside_far = swap(far_tile, 1)
    across_near, beside_far = tie((across_near, beside_far))
    corner_near = swap(across_near, 1)
    near_grad = pair_gradient(near_tile, beside_near, across_near, near_seen, ensemble)
    out, mid_grad = spread(
        (near_tile, near_grad, corner_near), (mid, mid_part, corner_mid), near, bands, fields.shape, ensemble
    )
    across_far, out = tie((across_far, out))
    corner_far = swap(across_far, 1)
    far_grad = pair_gradient(far_tile, beside_far, across_far, far_seen, ensemble)
    return spread((far_tile, far_grad, corner_far), mid_grad, far, bands, fields.shape, ensemble, out)


def solution(mesh):
    return jax.shard_map(
        shards,
        mesh=mesh,
        in_specs=(P("member", None, "band", None), P(None, "band", None)),
        out_specs=P("member", None, "band", None),
        check_vma=False,
    )
```

```python
import functools

import jax
import jax.numpy as jnp
import ml_dtypes
import numpy as np
from jax import lax
from jax.experimental import pallas as pl
from jax.experimental.pallas import tpu as pltpu
from jax.sharding import PartitionSpec as P

RADIUS = 16
SIGMA = 6.0
HUBER = 0.05
STRIDE = 4
MARGIN = RADIUS // STRIDE
LANES = 128
BLOCK = 256
TILE = 8
HALF = 32
NEAR = HALF // STRIDE + 2 * MARGIN
GROUP = 1
AHEAD = 3
VMEM = 40 * 1024 * 1024
WHOLE = 50 * 1024 * 1024


def kern(offset):
    taps = np.arange(-RADIUS, RADIUS + 1).astype(np.float64)
    norm = np.sum(np.exp(-taps * taps / (2.0 * SIGMA * SIGMA)))
    spot = np.asarray(offset).astype(np.float64)
    inside = np.abs(spot) <= RADIUS
    return np.where(inside, np.exp(-spot * spot / (2.0 * SIGMA * SIGMA)), 0.0) / norm


def parts(table):
    high = table.astype(np.float32).astype(ml_dtypes.bfloat16)
    low = (table - high.astype(np.float64)).astype(ml_dtypes.bfloat16)
    return high, low


def lon_offsets():
    lane = np.arange(LANES)
    even = np.where(lane < LANES - MARGIN, lane, lane - LANES)
    odd = np.where(lane < MARGIN, lane + LANES, lane) - LANES // 2
    fine = np.arange(BLOCK)
    return [fine[:, None] - STRIDE * place[None, :] for place in (even, odd)]


def spread_lon_table():
    pairs = [parts(kern(offset).T) for offset in lon_offsets()]
    return np.stack([np.concatenate([part, part], axis=0) for pair in pairs for part in pair])


def half_table():
    near = np.arange(NEAR) - MARGIN
    return kern(np.arange(HALF)[:, None] - STRIDE * near[None, :])


def per_image(table, images):
    eye = np.eye(images, dtype=np.float32)
    return np.kron(eye, table.astype(np.float32)).astype(ml_dtypes.bfloat16)


def spread_lat_table(images, scale):
    high, low = (per_image(part, images) for part in parts(scale * half_table()))
    return np.concatenate([high, high, low], axis=1)


def dot(a, b):
    return jnp.dot(a, b, preferred_element_type=jnp.float32)


def split(value):
    high = value.astype(jnp.bfloat16)
    low = (value - high.astype(jnp.float32)).astype(jnp.bfloat16)
    return high, low


def outside(shape, axis, band, bands, half):
    row = lax.broadcasted_iota(jnp.int32, shape, axis)
    above = (row < MARGIN) & (band == 0) & (half == 0)
    below = (row >= MARGIN) & (band == bands - 1) & (half == 1)
    return above | below


def taps(offset):
    norm = np.sum(np.exp(-np.arange(-RADIUS, RADIUS + 1).astype(np.float64) ** 2 / (2.0 * SIGMA * SIGMA)))
    spot = offset.astype(jnp.float32)
    value = jnp.exp(spot * spot * (-1.0 / (2.0 * SIGMA * SIGMA))) * (1.0 / norm)
    return jnp.where(jnp.abs(offset) <= RADIUS, value, 0.0)


def fill_thin_tables(lon_ref, lat_ref, variables, rows):
    shape = (BLOCK, LANES)
    fine = lax.broadcasted_iota(jnp.int32, shape, 0)
    lane = lax.broadcasted_iota(jnp.int32, shape, 1)
    even = jnp.where(lane < LANES - MARGIN, lane, lane - LANES)
    odd = jnp.where(lane < MARGIN, lane + LANES, lane) - LANES // 2
    for i, place in enumerate((even, odd)):
        high, low = split(taps(fine - STRIDE * place))
        lon_ref[i, :, :LANES] = high
        lon_ref[i, :, LANES:] = low
    near = rows // STRIDE + 2 * MARGIN
    depth = variables * rows
    shape = (variables * near, depth)
    out = lax.broadcasted_iota(jnp.int32, shape, 0)
    row = lax.broadcasted_iota(jnp.int32, shape, 1)
    image = sum((out >= v * near).astype(jnp.int32) for v in range(1, variables))
    offset = (row - image * rows) - STRIDE * (out - image * near - MARGIN)
    inside = (row >= image * rows) & (row < (image + 1) * rows)
    high, low = split(jnp.where(inside, taps(offset), 0.0))
    for part, value in enumerate((high, low)):
        place = pl.ds(part * variables * near, variables * near)
        lat_ref[place, :depth] = value
        lat_ref[place, depth:] = value


def thin_lon(value, lon_ref):
    variables, rows, length = value.shape
    value = value.reshape(variables * rows, length)
    count = length // BLOCK
    depth = value.shape[0]
    half = count // 2
    sums = [None] * count
    for odd in range(2):
        pairs = [split(value[:, k * BLOCK : (k + 1) * BLOCK]) for k in range(odd, count, 2)]
        stack = jnp.concatenate([p[0] for p in pairs] + [p[1] for p in pairs], axis=0)
        both = dot(stack, lon_ref[odd])
        both = both[:, :LANES] + both[:, LANES:]
        for i in range(half):
            sums[2 * i + odd] = (
                both[i * depth : (i + 1) * depth]
                + both[(half + i) * depth : (half + i + 1) * depth]
            )
    lane = lax.broadcasted_iota(jnp.int32, sums[0].shape, 1)
    zero = jnp.zeros_like(sums[0])
    columns = []
    for j in range(half):
        after = sums[2 * j + 2] if 2 * j + 2 < count else zero
        before = sums[2 * j - 1] if j > 0 else zero
        columns.append(
            jnp.where(lane >= LANES - MARGIN, after, sums[2 * j])
            + jnp.where(lane < MARGIN, before, sums[2 * j + 1])
        )
    high, low = split(jnp.concatenate(columns, axis=1))
    return jnp.concatenate([high, low], axis=0)


def thin_lat(stack, lat_ref, variables):
    both = dot(lat_ref[...], stack)
    middle = both.shape[0] // 2
    coarse = both[:middle] + both[middle:]
    return coarse.reshape(variables, 3, TILE, stack.shape[1])


def thin_kernel(bands, where_ref, x_ref, seen_hbm, near_ref, far_ref, mid_ref, held, lon_ref, lat_ref, seen_ref, arrived, seen_here):
    band = where_ref[0]
    even = band % 2 == 0
    members, variables, rows, _ = held.shape

    def copy(m):
        return pltpu.make_async_copy(x_ref.at[m], held.at[m], arrived.at[m])

    for m in range(AHEAD):
        copy(m).start()
    seen_copy = pltpu.make_async_copy(seen_hbm, seen_ref, seen_here)
    seen_copy.start()
    fill_thin_tables(lon_ref, lat_ref, variables, rows)
    def finish_rows(m, stack):
        coarse = thin_lat(stack, lat_ref, variables)
        upper, lower = coarse[:, 0], coarse[:, 2]
        upper = jnp.where(outside(upper.shape, 1, band, bands, 0), 0.0, upper)
        lower = jnp.where(outside(lower.shape, 1, band, bands, 1), 0.0, lower)
        near_ref[m] = jnp.where(even, lower, upper)
        far_ref[m] = jnp.where(even, upper, lower)
        mid_ref[m] = coarse[:, 1]

    before = None
    for m in range(members):
        copy(m).wait()
        if m + AHEAD < members:
            copy(m + AHEAD).start()
        stack = thin_lon(held[m], lon_ref)
        if m > 0:
            finish_rows(m - 1, before)
        before = stack
    finish_rows(members - 1, before)
    seen_copy.wait()
    seen = seen_ref[...]
    zero = jnp.zeros((seen.shape[0], MARGIN, seen.shape[2]), jnp.float32)
    upper = jnp.concatenate([zero, seen[:, :MARGIN]], axis=1)
    lower = jnp.concatenate([seen[:, -MARGIN:], zero], axis=1)
    near_ref[members] = jnp.where(even, lower, upper)
    far_ref[members] = jnp.where(even, upper, lower)


def thin(fields, observed, where, bands):
    members, variables, rows, length = fields.shape
    columns = length // STRIDE
    near = rows // STRIDE + 2 * MARGIN
    full = pl.BlockSpec(memory_space=pltpu.VMEM)
    any_space = pl.BlockSpec(memory_space=pl.ANY)
    edge = jax.ShapeDtypeStruct((members + 1, variables, TILE, columns), jnp.float32)
    return pl.pallas_call(
        functools.partial(thin_kernel, bands),
        in_specs=[pl.BlockSpec(memory_space=pltpu.SMEM), any_space, any_space],
        out_specs=[full] * 3,
        out_shape=[edge, edge, jax.ShapeDtypeStruct((members, variables, TILE, columns), jnp.float32)],
        scratch_shapes=[
            pltpu.VMEM(fields.shape, jnp.float32),
            pltpu.VMEM((2, BLOCK, 2 * LANES), jnp.bfloat16),
            pltpu.VMEM((2 * variables * near, 2 * variables * rows), jnp.bfloat16),
            pltpu.VMEM(observed.shape, jnp.float32),
            pltpu.SemaphoreType.DMA((members,)),
            pltpu.SemaphoreType.DMA,
        ],
        compiler_params=pltpu.CompilerParams(vmem_limit_bytes=WHOLE),
        cost_estimate=pl.CostEstimate(flops=1, bytes_accessed=1, transcendentals=0),
    )(where, fields, observed)


def soft_sign(diff):
    return diff * lax.rsqrt(diff * diff + HUBER * HUBER)


def pair_kernel(ensemble, own_ref, beside_ref, across_ref, seen_ref, out_ref):
    members, variables, _, columns = own_ref.shape
    tiles = columns // LANES

    def step(i, carry):
        v = i // tiles
        place = pl.ds(pl.multiple_of((i % tiles) * LANES, LANES), LANES)
        own = [own_ref[m, v, :, place] for m in range(members)]
        total = [None] * members
        for m in range(members):
            for n in range(m + 1, members):
                term = soft_sign(own[m] - own[n])
                total[m] = term if total[m] is None else total[m] + term
                total[n] = -term if total[n] is None else total[n] - term
        for other in (beside_ref, across_ref):
            for n in range(members):
                value = other[n, v, :, place]
                for m in range(members):
                    total[m] = total[m] + soft_sign(own[m] - value)
        seen = seen_ref[v, :, place]
        for m in range(members):
            out_ref[m, v, :, place] = soft_sign(own[m] - seen) * (1.0 / ensemble) - total[m] * (
                1.0 / (ensemble * (ensemble - 1))
            )
        return carry

    lax.fori_loop(0, variables * tiles, step, 0)


def pair_gradient(own, beside, across, seen, ensemble):
    full = pl.BlockSpec(memory_space=pltpu.VMEM)
    return pl.pallas_call(
        functools.partial(pair_kernel, ensemble),
        in_specs=[full] * 4,
        out_specs=full,
        out_shape=jax.ShapeDtypeStruct(own.shape, jnp.float32),
        compiler_params=pltpu.CompilerParams(vmem_limit_bytes=VMEM),
        cost_estimate=pl.CostEstimate(flops=1, bytes_accessed=1, transcendentals=0),
    )(own, beside, across, seen)


def finish(ensemble, group, own_ref, part_ref, corner_ref):
    own = own_ref[group]
    total = jnp.zeros_like(own)
    for n in range(corner_ref.shape[0]):
        total = total + soft_sign(own - corner_ref[n][None])
    return part_ref[group] - total * (1.0 / (ensemble * (ensemble - 1)))


def spread_lat(edge, mid, band, bands, half, lat_ref):
    group, variables, _, columns = edge.shape
    edge = jnp.where(outside(edge.shape, 2, band, bands, half), 0.0, edge)
    upper = jnp.where(half == 0, edge, mid)
    lower = jnp.where(half == 0, mid, edge)
    grad = jnp.stack([upper, lower], axis=2).reshape(group * variables * NEAR, columns)
    high, low = split(grad)
    return dot(lat_ref[...], jnp.concatenate([high, low, high], axis=0))


def spread_lon(tall, lon_ref, store):
    depth, columns = tall.shape
    tiles = [tall[:, j * LANES : (j + 1) * LANES] for j in range(columns // LANES)]
    lane = lax.broadcasted_iota(jnp.int32, tiles[0].shape, 1)
    zero = jnp.zeros_like(tiles[0])
    count = len(tiles)
    for odd in range(2):
        stacks = []
        for j in range(count):
            if odd:
                after = tiles[j + 1] if j + 1 < count else zero
                near = jnp.where(lane < MARGIN, after, tiles[j])
            else:
                before = tiles[j - 1] if j > 0 else zero
                near = jnp.where(lane >= LANES - MARGIN, before, tiles[j])
            stacks.append(jnp.concatenate(split(near), axis=1))
        stack = jnp.concatenate(stacks, axis=0)
        wide = dot(stack, lon_ref[2 * odd]) + dot(stack, lon_ref[2 * odd + 1])
        for j in range(count):
            store(2 * j + odd, wide[j * depth : (j + 1) * depth])


def spread_kernel(bands, ensemble, first, where_ref, *refs):
    if first:
        edge_trio, mid_trio = refs[:3], refs[3:6]
        lat_ref, lon_ref, out_ref, mid_ref, held, sent = refs[6:]
    else:
        edge_trio, mid_ref = refs[1:4], refs[4]
        lat_ref, lon_ref, out_ref, held, sent = refs[5:]
    band, half = where_ref[0], where_ref[1]
    members = held.shape[0]
    start = pl.multiple_of(half * HALF, HALF)

    def copy(c):
        group = pl.ds(c * GROUP, GROUP)
        return pltpu.make_async_copy(
            held.at[group], out_ref.at[group, :, pl.ds(start, HALF), :], sent.at[c]
        )

    def tall_rows(c):
        group = pl.ds(c * GROUP, GROUP)
        edge = finish(ensemble, group, *edge_trio)
        if first:
            mid = finish(ensemble, group, *mid_trio)
            mid_ref[group] = mid
        else:
            mid = mid_ref[group]
        return spread_lat(edge, mid, band, bands, half, lat_ref)

    chunks = members // GROUP
    after = tall_rows(0)
    for c in range(chunks):
        group = pl.ds(c * GROUP, GROUP)
        tall = after

        def store(k, value, group=group):
            shape = (GROUP, *held.shape[1:3], BLOCK)
            held[group, :, :, k * BLOCK : (k + 1) * BLOCK] = value.reshape(shape)

        if c + 1 < chunks:
            after = tall_rows(c + 1)
        spread_lon(tall, lon_ref, store)
        copy(c).start()
    for c in range(chunks):
        copy(c).wait()


def spread(edge, mid, where, bands, shape, ensemble, out=None):
    members, variables, _, length = shape
    lat = spread_lat_table(GROUP * variables, 64.0 * ensemble)
    lon = spread_lon_table()
    tile = jax.ShapeDtypeStruct(edge[0].shape, jnp.float32)
    whole = jax.ShapeDtypeStruct(shape, jnp.float32)
    full = pl.BlockSpec(memory_space=pltpu.VMEM)
    any_space = pl.BlockSpec(memory_space=pl.ANY)
    first = out is None
    operands = [*edge, *mid] if first else [out, *edge, mid]
    return pl.pallas_call(
        functools.partial(spread_kernel, bands, ensemble, first),
        in_specs=[pl.BlockSpec(memory_space=pltpu.SMEM)]
        + ([full] * 6 if first else [any_space] + [full] * 4)
        + [full] * 2,
        out_specs=[any_space, full] if first else any_space,
        out_shape=[whole, tile] if first else whole,
        scratch_shapes=[
            pltpu.VMEM((members, variables, HALF, length), jnp.float32),
            pltpu.SemaphoreType.DMA((members // GROUP,)),
        ],
        input_output_aliases={} if first else {1: 0},
        compiler_params=pltpu.CompilerParams(vmem_limit_bytes=VMEM),
        cost_estimate=pl.CostEstimate(flops=1, bytes_accessed=1, transcendentals=0),
    )(where, *operands, jnp.asarray(lat), jnp.asarray(lon))


def swap(value, bit):
    devices = lax.axis_size("member")
    return lax.ppermute(value, "member", [(i, i ^ bit) for i in range(devices)])


def pairs_of(bands, first):
    pairs = [(i, i + 1) for i in range(first, bands - 1, 2)]
    return pairs + [(j, i) for i, j in pairs]


def shards(fields, observed):
    members, _, rows, _ = fields.shape
    bands = lax.axis_size("band")
    ensemble = members * lax.axis_size("member")
    band = lax.axis_index("band").astype(jnp.int32)
    far = jnp.stack([band, band % 2])
    near = jnp.stack([band, 1 - band % 2])
    tie = lax.optimization_barrier
    near_part, far_part, mid = thin(fields, observed, band.reshape(1), bands)
    far_come = lax.ppermute(far_part, "band", pairs_of(bands, 1))
    near_come = lax.ppermute(near_part, "band", pairs_of(bands, 0))
    across_mid = swap(mid, 2)
    beside_mid = swap(mid, 1)
    near_tile = near_part[:members] + near_come[:members]
    near_seen = near_part[members] + near_come[members]
    across_near = swap(near_tile, 2)
    beside_near = swap(near_tile, 1)
    across_mid, near_tile = tie((across_mid, near_tile))
    corner_mid = swap(across_mid, 1)
    beside_mid, corner_mid = tie((beside_mid, corner_mid))
    mid_part = pair_gradient(mid, beside_mid, across_mid, observed[:, MARGIN:-MARGIN], ensemble)
    far_come, mid_part = tie((far_come, mid_part))
    far_tile = far_part[:members] + far_come[:members]
    far_seen = far_part[members] + far_come[members]
    across_far = swap(far_tile, 2)
    beside_far = swap(far_tile, 1)
    across_near, beside_far = tie((across_near, beside_far))
    corner_near = swap(across_near, 1)
    near_grad = pair_gradient(near_tile, beside_near, across_near, near_seen, ensemble)
    out, mid_grad = spread(
        (near_tile, near_grad, corner_near), (mid, mid_part, corner_mid), near, bands, fields.shape, ensemble
    )
    across_far, out = tie((across_far, out))
    corner_far = swap(across_far, 1)
    far_grad = pair_gradient(far_tile, beside_far, across_far, far_seen, ensemble)
    return spread((far_tile, far_grad, corner_far), mid_grad, far, bands, fields.shape, ensemble, out)


def solution(mesh):
    return jax.shard_map(
        shards,
        mesh=mesh,
        in_specs=(P("member", None, "band", None), P(None, "band", None)),
        out_specs=P("member", None, "band", None),
        check_vma=False,
    )
```

```python
import functools

import jax
import jax.numpy as jnp
import ml_dtypes
import numpy as np
from jax import lax
from jax.experimental import pallas as pl
from jax.experimental.pallas import tpu as pltpu
from jax.sharding import PartitionSpec as P

RADIUS = 16
SIGMA = 6.0
HUBER = 0.05
STRIDE = 4
MARGIN = RADIUS // STRIDE
LANES = 128
BLOCK = 256
TILE = 8
HALF = 32
NEAR = HALF // STRIDE + 2 * MARGIN
GROUP = 1
AHEAD = 3
VMEM = 40 * 1024 * 1024
WHOLE = 50 * 1024 * 1024


def kern(offset):
    taps = np.arange(-RADIUS, RADIUS + 1).astype(np.float64)
    norm = np.sum(np.exp(-taps * taps / (2.0 * SIGMA * SIGMA)))
    spot = np.asarray(offset).astype(np.float64)
    inside = np.abs(spot) <= RADIUS
    return np.where(inside, np.exp(-spot * spot / (2.0 * SIGMA * SIGMA)), 0.0) / norm


def parts(table):
    high = table.astype(np.float32).astype(ml_dtypes.bfloat16)
    low = (table - high.astype(np.float64)).astype(ml_dtypes.bfloat16)
    return high, low


def lon_offsets():
    lane = np.arange(LANES)
    even = np.where(lane < LANES - MARGIN, lane, lane - LANES)
    odd = np.where(lane < MARGIN, lane + LANES, lane) - LANES // 2
    fine = np.arange(BLOCK)
    return [fine[:, None] - STRIDE * place[None, :] for place in (even, odd)]


def spread_lon_table():
    pairs = [parts(kern(offset).T) for offset in lon_offsets()]
    return np.stack([np.concatenate([part, part], axis=0) for pair in pairs for part in pair])


def half_table():
    near = np.arange(NEAR) - MARGIN
    return kern(np.arange(HALF)[:, None] - STRIDE * near[None, :])


def per_image(table, images):
    eye = np.eye(images, dtype=np.float32)
    return np.kron(eye, table.astype(np.float32)).astype(ml_dtypes.bfloat16)


def spread_lat_table(images, scale):
    high, low = (per_image(part, images) for part in parts(scale * half_table()))
    return np.concatenate([high, high, low], axis=1)


def dot(a, b):
    return jnp.dot(a, b, preferred_element_type=jnp.float32)


def split(value):
    high = value.astype(jnp.bfloat16)
    low = (value - high.astype(jnp.float32)).astype(jnp.bfloat16)
    return high, low


def outside(shape, axis, band, bands, half):
    row = lax.broadcasted_iota(jnp.int32, shape, axis)
    above = (row < MARGIN) & (band == 0) & (half == 0)
    below = (row >= MARGIN) & (band == bands - 1) & (half == 1)
    return above | below


def taps(offset):
    norm = np.sum(np.exp(-np.arange(-RADIUS, RADIUS + 1).astype(np.float64) ** 2 / (2.0 * SIGMA * SIGMA)))
    spot = offset.astype(jnp.float32)
    value = jnp.exp(spot * spot * (-1.0 / (2.0 * SIGMA * SIGMA))) * (1.0 / norm)
    return jnp.where(jnp.abs(offset) <= RADIUS, value, 0.0)


def fill_thin_tables(lon_ref, lat_ref, variables, rows):
    shape = (BLOCK, LANES)
    fine = lax.broadcasted_iota(jnp.int32, shape, 0)
    lane = lax.broadcasted_iota(jnp.int32, shape, 1)
    even = jnp.where(lane < LANES - MARGIN, lane, lane - LANES)
    odd = jnp.where(lane < MARGIN, lane + LANES, lane) - LANES // 2
    for i, place in enumerate((even, odd)):
        high, low = split(taps(fine - STRIDE * place))
        lon_ref[i, :, :LANES] = high
        lon_ref[i, :, LANES:] = low
    near = rows // STRIDE + 2 * MARGIN
    depth = variables * rows
    shape = (variables * near, depth)
    out = lax.broadcasted_iota(jnp.int32, shape, 0)
    row = lax.broadcasted_iota(jnp.int32, shape, 1)
    image = sum((out >= v * near).astype(jnp.int32) for v in range(1, variables))
    offset = (row - image * rows) - STRIDE * (out - image * near - MARGIN)
    inside = (row >= image * rows) & (row < (image + 1) * rows)
    high, low = split(jnp.where(inside, taps(offset), 0.0))
    for part, value in enumerate((high, low)):
        place = pl.ds(part * variables * near, variables * near)
        lat_ref[place, :depth] = value
        lat_ref[place, depth:] = value


def thin_lon(value, lon_ref):
    variables, rows, length = value.shape
    value = value.reshape(variables * rows, length)
    count = length // BLOCK
    depth = value.shape[0]
    half = count // 2
    sums = [None] * count
    for odd in range(2):
        pairs = [split(value[:, k * BLOCK : (k + 1) * BLOCK]) for k in range(odd, count, 2)]
        stack = jnp.concatenate([p[0] for p in pairs] + [p[1] for p in pairs], axis=0)
        both = dot(stack, lon_ref[odd])
        both = both[:, :LANES] + both[:, LANES:]
        for i in range(half):
            sums[2 * i + odd] = (
                both[i * depth : (i + 1) * depth]
                + both[(half + i) * depth : (half + i + 1) * depth]
            )
    lane = lax.broadcasted_iota(jnp.int32, sums[0].shape, 1)
    zero = jnp.zeros_like(sums[0])
    columns = []
    for j in range(half):
        after = sums[2 * j + 2] if 2 * j + 2 < count else zero
        before = sums[2 * j - 1] if j > 0 else zero
        columns.append(
            jnp.where(lane >= LANES - MARGIN, after, sums[2 * j])
            + jnp.where(lane < MARGIN, before, sums[2 * j + 1])
        )
    high, low = split(jnp.concatenate(columns, axis=1))
    return jnp.concatenate([high, low], axis=0)


def thin_lat(stack, lat_ref, variables):
    both = dot(lat_ref[...], stack)
    middle = both.shape[0] // 2
    coarse = both[:middle] + both[middle:]
    return coarse.reshape(variables, 3, TILE, stack.shape[1])


def thin_kernel(bands, where_ref, x_ref, seen_hbm, near_ref, far_ref, mid_ref, held, lon_ref, lat_ref, seen_ref, arrived, seen_here):
    band = where_ref[0]
    even = band % 2 == 0
    members, variables, rows, _ = held.shape

    def copy(m):
        return pltpu.make_async_copy(x_ref.at[m], held.at[m], arrived.at[m])

    for m in range(AHEAD):
        copy(m).start()
    seen_copy = pltpu.make_async_copy(seen_hbm, seen_ref, seen_here)
    seen_copy.start()
    fill_thin_tables(lon_ref, lat_ref, variables, rows)
    def finish_rows(m, stack):
        coarse = thin_lat(stack, lat_ref, variables)
        upper, lower = coarse[:, 0], coarse[:, 2]
        upper = jnp.where(outside(upper.shape, 1, band, bands, 0), 0.0, upper)
        lower = jnp.where(outside(lower.shape, 1, band, bands, 1), 0.0, lower)
        near_ref[m] = jnp.where(even, lower, upper)
        far_ref[m] = jnp.where(even, upper, lower)
        mid_ref[m] = coarse[:, 1]

    before = None
    for m in range(members):
        copy(m).wait()
        if m + AHEAD < members:
            copy(m + AHEAD).start()
        stack = thin_lon(held[m], lon_ref)
        if m > 0:
            finish_rows(m - 1, before)
        before = stack
    finish_rows(members - 1, before)
    seen_copy.wait()
    seen = seen_ref[...]
    zero = jnp.zeros((seen.shape[0], MARGIN, seen.shape[2]), jnp.float32)
    upper = jnp.concatenate([zero, seen[:, :MARGIN]], axis=1)
    lower = jnp.concatenate([seen[:, -MARGIN:], zero], axis=1)
    near_ref[members] = jnp.where(even, lower, upper)
    far_ref[members] = jnp.where(even, upper, lower)


def thin(fields, observed, where, bands):
    members, variables, rows, length = fields.shape
    columns = length // STRIDE
    near = rows // STRIDE + 2 * MARGIN
    full = pl.BlockSpec(memory_space=pltpu.VMEM)
    any_space = pl.BlockSpec(memory_space=pl.ANY)
    edge = jax.ShapeDtypeStruct((members + 1, variables, TILE, columns), jnp.float32)
    return pl.pallas_call(
        functools.partial(thin_kernel, bands),
        in_specs=[pl.BlockSpec(memory_space=pltpu.SMEM), any_space, any_space],
        out_specs=[full] * 3,
        out_shape=[edge, edge, jax.ShapeDtypeStruct((members, variables, TILE, columns), jnp.float32)],
        scratch_shapes=[
            pltpu.VMEM(fields.shape, jnp.float32),
            pltpu.VMEM((2, BLOCK, 2 * LANES), jnp.bfloat16),
            pltpu.VMEM((2 * variables * near, 2 * variables * rows), jnp.bfloat16),
            pltpu.VMEM(observed.shape, jnp.float32),
            pltpu.SemaphoreType.DMA((members,)),
            pltpu.SemaphoreType.DMA,
        ],
        compiler_params=pltpu.CompilerParams(vmem_limit_bytes=WHOLE),
        cost_estimate=pl.CostEstimate(flops=1, bytes_accessed=1, transcendentals=0),
    )(where, fields, observed)


def soft_sign(diff):
    return diff * lax.rsqrt(diff * diff + HUBER * HUBER)


def pair_kernel(ensemble, own_ref, beside_ref, across_ref, seen_ref, out_ref):
    members, variables, _, columns = own_ref.shape
    tiles = columns // LANES

    def step(i, carry):
        v = i // tiles
        place = pl.ds(pl.multiple_of((i % tiles) * LANES, LANES), LANES)
        own = [own_ref[m, v, :, place] for m in range(members)]
        total = [None] * members
        for m in range(members):
            for n in range(m + 1, members):
                term = soft_sign(own[m] - own[n])
                total[m] = term if total[m] is None else total[m] + term
                total[n] = -term if total[n] is None else total[n] - term
        for other in (beside_ref, across_ref):
            for n in range(members):
                value = other[n, v, :, place]
                for m in range(members):
                    total[m] = total[m] + soft_sign(own[m] - value)
        seen = seen_ref[v, :, place]
        for m in range(members):
            out_ref[m, v, :, place] = soft_sign(own[m] - seen) * (1.0 / ensemble) - total[m] * (
                1.0 / (ensemble * (ensemble - 1))
            )
        return carry

    lax.fori_loop(0, variables * tiles, step, 0)


def pair_gradient(own, beside, across, seen, ensemble, moved=1):
    full = pl.BlockSpec(memory_space=pltpu.VMEM)
    return pl.pallas_call(
        functools.partial(pair_kernel, ensemble),
        in_specs=[full] * 4,
        out_specs=full,
        out_shape=jax.ShapeDtypeStruct(own.shape, jnp.float32),
        compiler_params=pltpu.CompilerParams(vmem_limit_bytes=VMEM),
        cost_estimate=pl.CostEstimate(flops=1, bytes_accessed=moved, transcendentals=0),
    )(own, beside, across, seen)


def finish(ensemble, group, own_ref, part_ref, corner_ref):
    own = own_ref[group]
    total = jnp.zeros_like(own)
    for n in range(corner_ref.shape[0]):
        total = total + soft_sign(own - corner_ref[n][None])
    return part_ref[group] - total * (1.0 / (ensemble * (ensemble - 1)))


def spread_lat(edge, mid, band, bands, half, lat_ref):
    group, variables, _, columns = edge.shape
    edge = jnp.where(outside(edge.shape, 2, band, bands, half), 0.0, edge)
    upper = jnp.where(half == 0, edge, mid)
    lower = jnp.where(half == 0, mid, edge)
    grad = jnp.stack([upper, lower], axis=2).reshape(group * variables * NEAR, columns)
    high, low = split(grad)
    return dot(lat_ref[...], jnp.concatenate([high, low, high], axis=0))


def spread_lon(tall, lon_ref, store):
    depth, columns = tall.shape
    tiles = [tall[:, j * LANES : (j + 1) * LANES] for j in range(columns // LANES)]
    lane = lax.broadcasted_iota(jnp.int32, tiles[0].shape, 1)
    zero = jnp.zeros_like(tiles[0])
    count = len(tiles)
    for odd in range(2):
        stacks = []
        for j in range(count):
            if odd:
                after = tiles[j + 1] if j + 1 < count else zero
                near = jnp.where(lane < MARGIN, after, tiles[j])
            else:
                before = tiles[j - 1] if j > 0 else zero
                near = jnp.where(lane >= LANES - MARGIN, before, tiles[j])
            stacks.append(jnp.concatenate(split(near), axis=1))
        stack = jnp.concatenate(stacks, axis=0)
        wide = dot(stack, lon_ref[2 * odd]) + dot(stack, lon_ref[2 * odd + 1])
        for j in range(count):
            store(2 * j + odd, wide[j * depth : (j + 1) * depth])


def spread_kernel(bands, ensemble, first, where_ref, *refs):
    if first:
        edge_trio, mid_trio = refs[:3], refs[3:6]
        lat_ref, lon_ref, out_ref, mid_ref, held, sent = refs[6:]
    else:
        edge_trio, mid_ref = refs[1:4], refs[4]
        lat_ref, lon_ref, out_ref, held, sent = refs[5:]
    band, half = where_ref[0], where_ref[1]
    members = held.shape[0]
    start = pl.multiple_of(half * HALF, HALF)

    def copy(c):
        group = pl.ds(c * GROUP, GROUP)
        return pltpu.make_async_copy(
            held.at[group], out_ref.at[group, :, pl.ds(start, HALF), :], sent.at[c]
        )

    def tall_rows(c):
        group = pl.ds(c * GROUP, GROUP)
        edge = finish(ensemble, group, *edge_trio)
        if first:
            mid = finish(ensemble, group, *mid_trio)
            mid_ref[group] = mid
        else:
            mid = mid_ref[group]
        return spread_lat(edge, mid, band, bands, half, lat_ref)

    chunks = members // GROUP
    after = tall_rows(0)
    for c in range(chunks):
        group = pl.ds(c * GROUP, GROUP)
        tall = after

        def store(k, value, group=group):
            shape = (GROUP, *held.shape[1:3], BLOCK)
            held[group, :, :, k * BLOCK : (k + 1) * BLOCK] = value.reshape(shape)

        if c + 1 < chunks:
            after = tall_rows(c + 1)
        spread_lon(tall, lon_ref, store)
        copy(c).start()
    for c in range(chunks):
        copy(c).wait()


def spread(edge, mid, where, bands, shape, ensemble, moved, out=None):
    members, variables, _, length = shape
    lat = spread_lat_table(GROUP * variables, 64.0 * ensemble)
    lon = spread_lon_table()
    tile = jax.ShapeDtypeStruct(edge[0].shape, jnp.float32)
    whole = jax.ShapeDtypeStruct(shape, jnp.float32)
    full = pl.BlockSpec(memory_space=pltpu.VMEM)
    any_space = pl.BlockSpec(memory_space=pl.ANY)
    first = out is None
    operands = [*edge, *mid] if first else [out, *edge, mid]
    return pl.pallas_call(
        functools.partial(spread_kernel, bands, ensemble, first),
        in_specs=[pl.BlockSpec(memory_space=pltpu.SMEM)]
        + ([full] * 6 if first else [any_space] + [full] * 4)
        + [full] * 2,
        out_specs=[any_space, full] if first else any_space,
        out_shape=[whole, tile] if first else whole,
        scratch_shapes=[
            pltpu.VMEM((members, variables, HALF, length), jnp.float32),
            pltpu.SemaphoreType.DMA((members // GROUP,)),
        ],
        input_output_aliases={} if first else {1: 0},
        compiler_params=pltpu.CompilerParams(vmem_limit_bytes=VMEM),
        cost_estimate=pl.CostEstimate(flops=1, bytes_accessed=moved, transcendentals=0),
    )(where, *operands, jnp.asarray(lat), jnp.asarray(lon))


def swap(value, bit):
    devices = lax.axis_size("member")
    return lax.ppermute(value, "member", [(i, i ^ bit) for i in range(devices)])


def pairs_of(bands, first):
    pairs = [(i, i + 1) for i in range(first, bands - 1, 2)]
    return pairs + [(j, i) for i, j in pairs]


def shards(fields, observed):
    members, _, rows, _ = fields.shape
    bands = lax.axis_size("band")
    ensemble = members * lax.axis_size("member")
    band = lax.axis_index("band").astype(jnp.int32)
    far = jnp.stack([band, band % 2])
    near = jnp.stack([band, 1 - band % 2])
    tie = lax.optimization_barrier
    with jax.named_scope("k_thin"):
        near_part, far_part, mid = thin(fields, observed, band.reshape(1), bands)
    with jax.named_scope("x_near"):
        near_come = lax.ppermute(near_part, "band", pairs_of(bands, 0))
    with jax.named_scope("x_ymid"):
        across_mid = swap(mid, 2)
    with jax.named_scope("x_cmid"):
        beside_mid = swap(mid, 1)
    with jax.named_scope("x_far"):
        far_come = lax.ppermute(far_part, "band", pairs_of(bands, 1))
    near_tile = near_part[:members] + near_come[:members]
    near_seen = near_part[members] + near_come[members]
    with jax.named_scope("x_ynear"):
        across_near = swap(near_tile, 2)
    with jax.named_scope("x_cnear"):
        beside_near = swap(near_tile, 1)
    across_mid, near_tile = tie((across_mid, near_tile))
    with jax.named_scope("x_dmid"):
        corner_mid = swap(across_mid, 1)
    beside_mid, corner_mid = tie((beside_mid, corner_mid))
    far_come, beside_near = tie((far_come, beside_near))
    far_tile = far_part[:members] + far_come[:members]
    far_seen = far_part[members] + far_come[members]
    with jax.named_scope("x_yfar"):
        across_far = swap(far_tile, 2)
    with jax.named_scope("x_cfar"):
        beside_far = swap(far_tile, 1)
    with jax.named_scope("k_pmid"):
        mid_part = pair_gradient(mid, beside_mid, across_mid, observed[:, MARGIN:-MARGIN], ensemble, 1)
    with jax.named_scope("x_dnear"):
        corner_near = swap(across_near, 1)
    with jax.named_scope("k_pnear"):
        near_grad = pair_gradient(near_tile, beside_near, across_near, near_seen, ensemble, 1)
    trio = (near_tile, near_grad, corner_near)
    with jax.named_scope("k_near"):
        out, mid_grad = spread(trio, (mid, mid_part, corner_mid), near, bands, fields.shape, ensemble, 8000000)
    across_far, out = tie((across_far, out))
    with jax.named_scope("x_dfar"):
        corner_far = swap(across_far, 1)
    with jax.named_scope("k_pfar"):
        far_grad = pair_gradient(far_tile, beside_far, across_far, far_seen, ensemble, 1)
    trio = (far_tile, far_grad, corner_far)
    with jax.named_scope("k_far"):
        out = spread(trio, mid_grad, far, bands, fields.shape, ensemble, 1, out)
    return out


def solution(mesh):
    return jax.shard_map(
        shards,
        mesh=mesh,
        in_specs=(P("member", None, "band", None), P(None, "band", None)),
        out_specs=P("member", None, "band", None),
        check_vma=False,
    )
```

```python
import functools

import jax
import jax.numpy as jnp
import ml_dtypes
import numpy as np
from jax import lax
from jax.experimental import pallas as pl
from jax.experimental.pallas import tpu as pltpu
from jax.sharding import PartitionSpec as P

RADIUS = 16
SIGMA = 6.0
HUBER = 0.05
STRIDE = 4
MARGIN = RADIUS // STRIDE
LANES = 128
BLOCK = 256
TILE = 8
HALF = 32
NEAR = HALF // STRIDE + 2 * MARGIN
GROUP = 1
AHEAD = 3
VMEM = 40 * 1024 * 1024
WHOLE = 50 * 1024 * 1024


def kern(offset):
    taps = np.arange(-RADIUS, RADIUS + 1).astype(np.float64)
    norm = np.sum(np.exp(-taps * taps / (2.0 * SIGMA * SIGMA)))
    spot = np.asarray(offset).astype(np.float64)
    inside = np.abs(spot) <= RADIUS
    return np.where(inside, np.exp(-spot * spot / (2.0 * SIGMA * SIGMA)), 0.0) / norm


def parts(table):
    high = table.astype(np.float32).astype(ml_dtypes.bfloat16)
    low = (table - high.astype(np.float64)).astype(ml_dtypes.bfloat16)
    return high, low


def lon_offsets():
    lane = np.arange(LANES)
    even = np.where(lane < LANES - MARGIN, lane, lane - LANES)
    odd = np.where(lane < MARGIN, lane + LANES, lane) - LANES // 2
    fine = np.arange(BLOCK)
    return [fine[:, None] - STRIDE * place[None, :] for place in (even, odd)]


def spread_lon_table():
    pairs = [parts(kern(offset).T) for offset in lon_offsets()]
    return np.stack([np.concatenate([part, part], axis=0) for pair in pairs for part in pair])


def half_table():
    near = np.arange(NEAR) - MARGIN
    return kern(np.arange(HALF)[:, None] - STRIDE * near[None, :])


def per_image(table, images):
    eye = np.eye(images, dtype=np.float32)
    return np.kron(eye, table.astype(np.float32)).astype(ml_dtypes.bfloat16)


def spread_lat_table(images, scale):
    high, low = (per_image(part, images) for part in parts(scale * half_table()))
    return np.concatenate([high, high, low], axis=1)


def dot(a, b):
    return jnp.dot(a, b, preferred_element_type=jnp.float32)


def split(value):
    high = value.astype(jnp.bfloat16)
    low = (value - high.astype(jnp.float32)).astype(jnp.bfloat16)
    return high, low


def outside(shape, axis, band, bands, half):
    row = lax.broadcasted_iota(jnp.int32, shape, axis)
    above = (row < MARGIN) & (band == 0) & (half == 0)
    below = (row >= MARGIN) & (band == bands - 1) & (half == 1)
    return above | below


def taps(offset):
    norm = np.sum(np.exp(-np.arange(-RADIUS, RADIUS + 1).astype(np.float64) ** 2 / (2.0 * SIGMA * SIGMA)))
    spot = offset.astype(jnp.float32)
    value = jnp.exp(spot * spot * (-1.0 / (2.0 * SIGMA * SIGMA))) * (1.0 / norm)
    return jnp.where(jnp.abs(offset) <= RADIUS, value, 0.0)


def fill_thin_tables(lon_ref, lat_ref, variables, rows):
    shape = (BLOCK, LANES)
    fine = lax.broadcasted_iota(jnp.int32, shape, 0)
    lane = lax.broadcasted_iota(jnp.int32, shape, 1)
    even = jnp.where(lane < LANES - MARGIN, lane, lane - LANES)
    odd = jnp.where(lane < MARGIN, lane + LANES, lane) - LANES // 2
    for i, place in enumerate((even, odd)):
        high, low = split(taps(fine - STRIDE * place))
        lon_ref[i, :, :LANES] = high
        lon_ref[i, :, LANES:] = low
    near = rows // STRIDE + 2 * MARGIN
    depth = variables * rows
    shape = (variables * near, depth)
    out = lax.broadcasted_iota(jnp.int32, shape, 0)
    row = lax.broadcasted_iota(jnp.int32, shape, 1)
    image = sum((out >= v * near).astype(jnp.int32) for v in range(1, variables))
    offset = (row - image * rows) - STRIDE * (out - image * near - MARGIN)
    inside = (row >= image * rows) & (row < (image + 1) * rows)
    high, low = split(jnp.where(inside, taps(offset), 0.0))
    for part, value in enumerate((high, low)):
        place = pl.ds(part * variables * near, variables * near)
        lat_ref[place, :depth] = value
        lat_ref[place, depth:] = value


def thin_lon(value, lon_ref):
    variables, rows, length = value.shape
    value = value.reshape(variables * rows, length)
    count = length // BLOCK
    depth = value.shape[0]
    half = count // 2
    sums = [None] * count
    for odd in range(2):
        pairs = [split(value[:, k * BLOCK : (k + 1) * BLOCK]) for k in range(odd, count, 2)]
        stack = jnp.concatenate([p[0] for p in pairs] + [p[1] for p in pairs], axis=0)
        both = dot(stack, lon_ref[odd])
        both = both[:, :LANES] + both[:, LANES:]
        for i in range(half):
            sums[2 * i + odd] = (
                both[i * depth : (i + 1) * depth]
                + both[(half + i) * depth : (half + i + 1) * depth]
            )
    lane = lax.broadcasted_iota(jnp.int32, sums[0].shape, 1)
    zero = jnp.zeros_like(sums[0])
    columns = []
    for j in range(half):
        after = sums[2 * j + 2] if 2 * j + 2 < count else zero
        before = sums[2 * j - 1] if j > 0 else zero
        columns.append(
            jnp.where(lane >= LANES - MARGIN, after, sums[2 * j])
            + jnp.where(lane < MARGIN, before, sums[2 * j + 1])
        )
    high, low = split(jnp.concatenate(columns, axis=1))
    return jnp.concatenate([high, low], axis=0)


def thin_lat(stack, lat_ref, variables):
    both = dot(lat_ref[...], stack)
    middle = both.shape[0] // 2
    coarse = both[:middle] + both[middle:]
    return coarse.reshape(variables, 3, TILE, stack.shape[1])


def thin_kernel(bands, where_ref, x_ref, seen_hbm, near_ref, far_ref, mid_ref, held, lon_ref, lat_ref, seen_ref, arrived, seen_here):
    band = where_ref[0]
    even = band % 2 == 0
    members, variables, rows, _ = held.shape

    def copy(m):
        return pltpu.make_async_copy(x_ref.at[m], held.at[m], arrived.at[m])

    for m in range(AHEAD):
        copy(m).start()
    seen_copy = pltpu.make_async_copy(seen_hbm, seen_ref, seen_here)
    seen_copy.start()
    fill_thin_tables(lon_ref, lat_ref, variables, rows)
    def finish_rows(m, stack):
        coarse = thin_lat(stack, lat_ref, variables)
        upper, lower = coarse[:, 0], coarse[:, 2]
        upper = jnp.where(outside(upper.shape, 1, band, bands, 0), 0.0, upper)
        lower = jnp.where(outside(lower.shape, 1, band, bands, 1), 0.0, lower)
        near_ref[m] = jnp.where(even, lower, upper)
        far_ref[m] = jnp.where(even, upper, lower)
        mid_ref[m] = coarse[:, 1]

    before = None
    for m in range(members):
        copy(m).wait()
        if m + AHEAD < members:
            copy(m + AHEAD).start()
        stack = thin_lon(held[m], lon_ref)
        if m > 0:
            finish_rows(m - 1, before)
        before = stack
    finish_rows(members - 1, before)
    seen_copy.wait()
    seen = seen_ref[...]
    zero = jnp.zeros((seen.shape[0], MARGIN, seen.shape[2]), jnp.float32)
    upper = jnp.concatenate([zero, seen[:, :MARGIN]], axis=1)
    lower = jnp.concatenate([seen[:, -MARGIN:], zero], axis=1)
    near_ref[members] = jnp.where(even, lower, upper)
    far_ref[members] = jnp.where(even, upper, lower)


def thin(fields, observed, where, bands):
    members, variables, rows, length = fields.shape
    columns = length // STRIDE
    near = rows // STRIDE + 2 * MARGIN
    full = pl.BlockSpec(memory_space=pltpu.VMEM)
    any_space = pl.BlockSpec(memory_space=pl.ANY)
    edge = jax.ShapeDtypeStruct((members + 1, variables, TILE, columns), jnp.float32)
    return pl.pallas_call(
        functools.partial(thin_kernel, bands),
        in_specs=[pl.BlockSpec(memory_space=pltpu.SMEM), any_space, any_space],
        out_specs=[full] * 3,
        out_shape=[edge, edge, jax.ShapeDtypeStruct((members, variables, TILE, columns), jnp.float32)],
        scratch_shapes=[
            pltpu.VMEM(fields.shape, jnp.float32),
            pltpu.VMEM((2, BLOCK, 2 * LANES), jnp.bfloat16),
            pltpu.VMEM((2 * variables * near, 2 * variables * rows), jnp.bfloat16),
            pltpu.VMEM(observed.shape, jnp.float32),
            pltpu.SemaphoreType.DMA((members,)),
            pltpu.SemaphoreType.DMA,
        ],
        compiler_params=pltpu.CompilerParams(vmem_limit_bytes=WHOLE),
        cost_estimate=pl.CostEstimate(flops=1, bytes_accessed=1, transcendentals=0),
    )(where, fields, observed)


def soft_sign(diff):
    return diff * lax.rsqrt(diff * diff + HUBER * HUBER)


def pair_kernel(ensemble, own_ref, beside_ref, across_ref, seen_ref, out_ref):
    members, variables, _, columns = own_ref.shape
    tiles = columns // LANES

    def step(i, carry):
        v = i // tiles
        place = pl.ds(pl.multiple_of((i % tiles) * LANES, LANES), LANES)
        own = [own_ref[m, v, :, place] for m in range(members)]
        total = [None] * members
        for m in range(members):
            for n in range(m + 1, members):
                term = soft_sign(own[m] - own[n])
                total[m] = term if total[m] is None else total[m] + term
                total[n] = -term if total[n] is None else total[n] - term
        for other in (beside_ref, across_ref):
            for n in range(members):
                value = other[n, v, :, place]
                for m in range(members):
                    total[m] = total[m] + soft_sign(own[m] - value)
        seen = seen_ref[v, :, place]
        for m in range(members):
            out_ref[m, v, :, place] = soft_sign(own[m] - seen) * (1.0 / ensemble) - total[m] * (
                1.0 / (ensemble * (ensemble - 1))
            )
        return carry

    lax.fori_loop(0, variables * tiles, step, 0)


def pair_gradient(own, beside, across, seen, ensemble, moved=1):
    full = pl.BlockSpec(memory_space=pltpu.VMEM)
    return pl.pallas_call(
        functools.partial(pair_kernel, ensemble),
        in_specs=[full] * 4,
        out_specs=full,
        out_shape=jax.ShapeDtypeStruct(own.shape, jnp.float32),
        compiler_params=pltpu.CompilerParams(vmem_limit_bytes=VMEM),
        cost_estimate=pl.CostEstimate(flops=1, bytes_accessed=moved, transcendentals=0),
    )(own, beside, across, seen)


def finish(ensemble, group, own_ref, part_ref, corner_ref):
    own = own_ref[group]
    total = jnp.zeros_like(own)
    for n in range(corner_ref.shape[0]):
        total = total + soft_sign(own - corner_ref[n][None])
    return part_ref[group] - total * (1.0 / (ensemble * (ensemble - 1)))


def spread_lat(edge, mid, band, bands, half, lat_ref):
    group, variables, _, columns = edge.shape
    edge = jnp.where(outside(edge.shape, 2, band, bands, half), 0.0, edge)
    upper = jnp.where(half == 0, edge, mid)
    lower = jnp.where(half == 0, mid, edge)
    grad = jnp.stack([upper, lower], axis=2).reshape(group * variables * NEAR, columns)
    high, low = split(grad)
    return dot(lat_ref[...], jnp.concatenate([high, low, high], axis=0))


def spread_lon(tall, lon_ref, store):
    depth, columns = tall.shape
    tiles = [tall[:, j * LANES : (j + 1) * LANES] for j in range(columns // LANES)]
    lane = lax.broadcasted_iota(jnp.int32, tiles[0].shape, 1)
    zero = jnp.zeros_like(tiles[0])
    count = len(tiles)
    for odd in range(2):
        stacks = []
        for j in range(count):
            if odd:
                after = tiles[j + 1] if j + 1 < count else zero
                near = jnp.where(lane < MARGIN, after, tiles[j])
            else:
                before = tiles[j - 1] if j > 0 else zero
                near = jnp.where(lane >= LANES - MARGIN, before, tiles[j])
            stacks.append(jnp.concatenate(split(near), axis=1))
        stack = jnp.concatenate(stacks, axis=0)
        wide = dot(stack, lon_ref[2 * odd]) + dot(stack, lon_ref[2 * odd + 1])
        for j in range(count):
            store(2 * j + odd, wide[j * depth : (j + 1) * depth])


def spread_kernel(bands, ensemble, first, where_ref, *refs):
    if first:
        edge_trio, mid_trio = refs[:3], refs[3:6]
        lat_ref, lon_ref, out_ref, mid_ref, held, sent = refs[6:]
    else:
        edge_trio, mid_ref = refs[1:4], refs[4]
        lat_ref, lon_ref, out_ref, held, sent = refs[5:]
    band, half = where_ref[0], where_ref[1]
    members = held.shape[0]
    start = pl.multiple_of(half * HALF, HALF)

    def copy(c):
        group = pl.ds(c * GROUP, GROUP)
        return pltpu.make_async_copy(
            held.at[group], out_ref.at[group, :, pl.ds(start, HALF), :], sent.at[c]
        )

    def tall_rows(c):
        group = pl.ds(c * GROUP, GROUP)
        edge = finish(ensemble, group, *edge_trio)
        if first:
            mid = finish(ensemble, group, *mid_trio)
            mid_ref[group] = mid
        else:
            mid = mid_ref[group]
        return spread_lat(edge, mid, band, bands, half, lat_ref)

    chunks = members // GROUP
    after = tall_rows(0)
    for c in range(chunks):
        group = pl.ds(c * GROUP, GROUP)
        tall = after

        def store(k, value, group=group):
            shape = (GROUP, *held.shape[1:3], BLOCK)
            held[group, :, :, k * BLOCK : (k + 1) * BLOCK] = value.reshape(shape)

        if c + 1 < chunks:
            after = tall_rows(c + 1)
        spread_lon(tall, lon_ref, store)
        copy(c).start()
    for c in range(chunks):
        copy(c).wait()


def spread(edge, mid, where, bands, shape, ensemble, moved, out=None):
    members, variables, _, length = shape
    lat = spread_lat_table(GROUP * variables, 64.0 * ensemble)
    lon = spread_lon_table()
    tile = jax.ShapeDtypeStruct(edge[0].shape, jnp.float32)
    whole = jax.ShapeDtypeStruct(shape, jnp.float32)
    full = pl.BlockSpec(memory_space=pltpu.VMEM)
    any_space = pl.BlockSpec(memory_space=pl.ANY)
    first = out is None
    operands = [*edge, *mid] if first else [out, *edge, mid]
    return pl.pallas_call(
        functools.partial(spread_kernel, bands, ensemble, first),
        in_specs=[pl.BlockSpec(memory_space=pltpu.SMEM)]
        + ([full] * 6 if first else [any_space] + [full] * 4)
        + [full] * 2,
        out_specs=[any_space, full] if first else any_space,
        out_shape=[whole, tile] if first else whole,
        scratch_shapes=[
            pltpu.VMEM((members, variables, HALF, length), jnp.float32),
            pltpu.SemaphoreType.DMA((members // GROUP,)),
        ],
        input_output_aliases={} if first else {1: 0},
        compiler_params=pltpu.CompilerParams(vmem_limit_bytes=VMEM),
        cost_estimate=pl.CostEstimate(flops=1, bytes_accessed=moved, transcendentals=0),
    )(where, *operands, jnp.asarray(lat), jnp.asarray(lon))


def swap(value, bit):
    devices = lax.axis_size("member")
    return lax.ppermute(value, "member", [(i, i ^ bit) for i in range(devices)])


def pairs_of(bands, first):
    pairs = [(i, i + 1) for i in range(first, bands - 1, 2)]
    return pairs + [(j, i) for i, j in pairs]


def shards(fields, observed):
    members, _, rows, _ = fields.shape
    bands = lax.axis_size("band")
    ensemble = members * lax.axis_size("member")
    band = lax.axis_index("band").astype(jnp.int32)
    far = jnp.stack([band, band % 2])
    near = jnp.stack([band, 1 - band % 2])
    tie = lax.optimization_barrier
    with jax.named_scope("k_thin"):
        near_part, far_part, mid = thin(fields, observed, band.reshape(1), bands)
    with jax.named_scope("x_near"):
        near_come = lax.ppermute(near_part, "band", pairs_of(bands, 0))
    with jax.named_scope("x_ymid"):
        across_mid = swap(mid, 2)
    with jax.named_scope("x_cmid"):
        beside_mid = swap(mid, 1)
    with jax.named_scope("x_far"):
        far_come = lax.ppermute(far_part, "band", pairs_of(bands, 1))
    near_tile = near_part[:members] + near_come[:members]
    near_seen = near_part[members] + near_come[members]
    with jax.named_scope("x_ynear"):
        across_near = swap(near_tile, 2)
    with jax.named_scope("x_cnear"):
        beside_near = swap(near_tile, 1)
    across_mid, near_tile = tie((across_mid, near_tile))
    with jax.named_scope("x_dmid"):
        corner_mid = swap(across_mid, 1)
    with jax.named_scope("k_pmid"):
        mid_part = pair_gradient(mid, beside_mid, across_mid, observed[:, MARGIN:-MARGIN], ensemble, 1)
    far_come, mid_part = tie((far_come, mid_part))
    far_come, beside_near = tie((far_come, beside_near))
    far_tile = far_part[:members] + far_come[:members]
    far_seen = far_part[members] + far_come[members]
    with jax.named_scope("x_yfar"):
        across_far = swap(far_tile, 2)
    with jax.named_scope("x_cfar"):
        beside_far = swap(far_tile, 1)
    with jax.named_scope("x_dnear"):
        corner_near = swap(across_near, 1)
    with jax.named_scope("k_pnear"):
        near_grad = pair_gradient(near_tile, beside_near, across_near, near_seen, ensemble, 1)
    trio = (near_tile, near_grad, corner_near)
    with jax.named_scope("k_near"):
        out, mid_grad = spread(trio, (mid, mid_part, corner_mid), near, bands, fields.shape, ensemble, 8000000)
    across_far, out = tie((across_far, out))
    with jax.named_scope("x_dfar"):
        corner_far = swap(across_far, 1)
    with jax.named_scope("k_pfar"):
        far_grad = pair_gradient(far_tile, beside_far, across_far, far_seen, ensemble, 1)
    trio = (far_tile, far_grad, corner_far)
    with jax.named_scope("k_far"):
        out = spread(trio, mid_grad, far, bands, fields.shape, ensemble, 1, out)
    return out


def solution(mesh):
    return jax.shard_map(
        shards,
        mesh=mesh,
        in_specs=(P("member", None, "band", None), P(None, "band", None)),
        out_specs=P("member", None, "band", None),
        check_vma=False,
    )
```

```python
import functools

import jax
import jax.numpy as jnp
import ml_dtypes
import numpy as np
from jax import lax
from jax.experimental import pallas as pl
from jax.experimental.pallas import tpu as pltpu
from jax.sharding import PartitionSpec as P

RADIUS = 16
SIGMA = 6.0
HUBER = 0.05
STRIDE = 4
MARGIN = RADIUS // STRIDE
LANES = 128
BLOCK = 256
TILE = 8
HALF = 32
NEAR = HALF // STRIDE + 2 * MARGIN
GROUP = 1
AHEAD = 3
VMEM = 40 * 1024 * 1024
WHOLE = 50 * 1024 * 1024


def kern(offset):
    taps = np.arange(-RADIUS, RADIUS + 1).astype(np.float64)
    norm = np.sum(np.exp(-taps * taps / (2.0 * SIGMA * SIGMA)))
    spot = np.asarray(offset).astype(np.float64)
    inside = np.abs(spot) <= RADIUS
    return np.where(inside, np.exp(-spot * spot / (2.0 * SIGMA * SIGMA)), 0.0) / norm


def parts(table):
    high = table.astype(np.float32).astype(ml_dtypes.bfloat16)
    low = (table - high.astype(np.float64)).astype(ml_dtypes.bfloat16)
    return high, low


def lon_offsets():
    lane = np.arange(LANES)
    even = np.where(lane < LANES - MARGIN, lane, lane - LANES)
    odd = np.where(lane < MARGIN, lane + LANES, lane) - LANES // 2
    fine = np.arange(BLOCK)
    return [fine[:, None] - STRIDE * place[None, :] for place in (even, odd)]


def spread_lon_table():
    pairs = [parts(kern(offset).T) for offset in lon_offsets()]
    return np.stack([np.concatenate([part, part], axis=0) for pair in pairs for part in pair])


def half_table():
    near = np.arange(NEAR) - MARGIN
    return kern(np.arange(HALF)[:, None] - STRIDE * near[None, :])


def per_image(table, images):
    eye = np.eye(images, dtype=np.float32)
    return np.kron(eye, table.astype(np.float32)).astype(ml_dtypes.bfloat16)


def spread_lat_table(images, scale):
    high, low = (per_image(part, images) for part in parts(scale * half_table()))
    return np.concatenate([high, high, low], axis=1)


def dot(a, b):
    return jnp.dot(a, b, preferred_element_type=jnp.float32)


def split(value):
    high = value.astype(jnp.bfloat16)
    low = (value - high.astype(jnp.float32)).astype(jnp.bfloat16)
    return high, low


def outside(shape, axis, band, bands, half):
    row = lax.broadcasted_iota(jnp.int32, shape, axis)
    above = (row < MARGIN) & (band == 0) & (half == 0)
    below = (row >= MARGIN) & (band == bands - 1) & (half == 1)
    return above | below


def taps(offset):
    norm = np.sum(np.exp(-np.arange(-RADIUS, RADIUS + 1).astype(np.float64) ** 2 / (2.0 * SIGMA * SIGMA)))
    spot = offset.astype(jnp.float32)
    value = jnp.exp(spot * spot * (-1.0 / (2.0 * SIGMA * SIGMA))) * (1.0 / norm)
    return jnp.where(jnp.abs(offset) <= RADIUS, value, 0.0)


def fill_thin_tables(lon_ref, lat_ref, variables, rows):
    shape = (BLOCK, LANES)
    fine = lax.broadcasted_iota(jnp.int32, shape, 0)
    lane = lax.broadcasted_iota(jnp.int32, shape, 1)
    even = jnp.where(lane < LANES - MARGIN, lane, lane - LANES)
    odd = jnp.where(lane < MARGIN, lane + LANES, lane) - LANES // 2
    for i, place in enumerate((even, odd)):
        high, low = split(taps(fine - STRIDE * place))
        lon_ref[i, :, :LANES] = high
        lon_ref[i, :, LANES:] = low
    near = rows // STRIDE + 2 * MARGIN
    depth = variables * rows
    shape = (variables * near, depth)
    out = lax.broadcasted_iota(jnp.int32, shape, 0)
    row = lax.broadcasted_iota(jnp.int32, shape, 1)
    image = sum((out >= v * near).astype(jnp.int32) for v in range(1, variables))
    offset = (row - image * rows) - STRIDE * (out - image * near - MARGIN)
    inside = (row >= image * rows) & (row < (image + 1) * rows)
    high, low = split(jnp.where(inside, taps(offset), 0.0))
    for part, value in enumerate((high, low)):
        place = pl.ds(part * variables * near, variables * near)
        lat_ref[place, :depth] = value
        lat_ref[place, depth:] = value


def thin_lon(value, lon_ref):
    variables, rows, length = value.shape
    value = value.reshape(variables * rows, length)
    count = length // BLOCK
    depth = value.shape[0]
    half = count // 2
    sums = [None] * count
    for odd in range(2):
        pairs = [split(value[:, k * BLOCK : (k + 1) * BLOCK]) for k in range(odd, count, 2)]
        stack = jnp.concatenate([p[0] for p in pairs] + [p[1] for p in pairs], axis=0)
        both = dot(stack, lon_ref[odd])
        both = both[:, :LANES] + both[:, LANES:]
        for i in range(half):
            sums[2 * i + odd] = (
                both[i * depth : (i + 1) * depth]
                + both[(half + i) * depth : (half + i + 1) * depth]
            )
    lane = lax.broadcasted_iota(jnp.int32, sums[0].shape, 1)
    zero = jnp.zeros_like(sums[0])
    columns = []
    for j in range(half):
        after = sums[2 * j + 2] if 2 * j + 2 < count else zero
        before = sums[2 * j - 1] if j > 0 else zero
        columns.append(
            jnp.where(lane >= LANES - MARGIN, after, sums[2 * j])
            + jnp.where(lane < MARGIN, before, sums[2 * j + 1])
        )
    high, low = split(jnp.concatenate(columns, axis=1))
    return jnp.concatenate([high, low], axis=0)


def thin_lat(stack, lat_ref, variables):
    both = dot(lat_ref[...], stack)
    middle = both.shape[0] // 2
    coarse = both[:middle] + both[middle:]
    return coarse.reshape(variables, 3, TILE, stack.shape[1])


def thin_kernel(bands, where_ref, x_ref, seen_hbm, near_ref, far_ref, mid_ref, held, lon_ref, lat_ref, seen_ref, arrived, seen_here):
    band = where_ref[0]
    even = band % 2 == 0
    members, variables, rows, _ = held.shape

    def copy(m):
        return pltpu.make_async_copy(x_ref.at[m], held.at[m], arrived.at[m])

    for m in range(AHEAD):
        copy(m).start()
    seen_copy = pltpu.make_async_copy(seen_hbm, seen_ref, seen_here)
    seen_copy.start()
    fill_thin_tables(lon_ref, lat_ref, variables, rows)
    def finish_rows(m, stack):
        coarse = thin_lat(stack, lat_ref, variables)
        upper, lower = coarse[:, 0], coarse[:, 2]
        upper = jnp.where(outside(upper.shape, 1, band, bands, 0), 0.0, upper)
        lower = jnp.where(outside(lower.shape, 1, band, bands, 1), 0.0, lower)
        near_ref[m] = jnp.where(even, lower, upper)
        far_ref[m] = jnp.where(even, upper, lower)
        mid_ref[m] = coarse[:, 1]

    before = None
    for m in range(members):
        copy(m).wait()
        if m + AHEAD < members:
            copy(m + AHEAD).start()
        stack = thin_lon(held[m], lon_ref)
        if m > 0:
            finish_rows(m - 1, before)
        before = stack
    finish_rows(members - 1, before)
    seen_copy.wait()
    seen = seen_ref[...]
    zero = jnp.zeros((seen.shape[0], MARGIN, seen.shape[2]), jnp.float32)
    upper = jnp.concatenate([zero, seen[:, :MARGIN]], axis=1)
    lower = jnp.concatenate([seen[:, -MARGIN:], zero], axis=1)
    near_ref[members] = jnp.where(even, lower, upper)
    far_ref[members] = jnp.where(even, upper, lower)


def thin(fields, observed, where, bands):
    members, variables, rows, length = fields.shape
    columns = length // STRIDE
    near = rows // STRIDE + 2 * MARGIN
    full = pl.BlockSpec(memory_space=pltpu.VMEM)
    any_space = pl.BlockSpec(memory_space=pl.ANY)
    edge = jax.ShapeDtypeStruct((members + 1, variables, TILE, columns), jnp.float32)
    return pl.pallas_call(
        functools.partial(thin_kernel, bands),
        in_specs=[pl.BlockSpec(memory_space=pltpu.SMEM), any_space, any_space],
        out_specs=[full] * 3,
        out_shape=[edge, edge, jax.ShapeDtypeStruct((members, variables, TILE, columns), jnp.float32)],
        scratch_shapes=[
            pltpu.VMEM(fields.shape, jnp.float32),
            pltpu.VMEM((2, BLOCK, 2 * LANES), jnp.bfloat16),
            pltpu.VMEM((2 * variables * near, 2 * variables * rows), jnp.bfloat16),
            pltpu.VMEM(observed.shape, jnp.float32),
            pltpu.SemaphoreType.DMA((members,)),
            pltpu.SemaphoreType.DMA,
        ],
        compiler_params=pltpu.CompilerParams(vmem_limit_bytes=WHOLE),
        cost_estimate=pl.CostEstimate(flops=1, bytes_accessed=1, transcendentals=0),
    )(where, fields, observed)


def soft_sign(diff):
    return diff * lax.rsqrt(diff * diff + HUBER * HUBER)


def pair_kernel(ensemble, own_ref, beside_ref, across_ref, seen_ref, out_ref):
    members, variables, _, columns = own_ref.shape
    tiles = columns // LANES

    def step(i, carry):
        v = i // tiles
        place = pl.ds(pl.multiple_of((i % tiles) * LANES, LANES), LANES)
        own = [own_ref[m, v, :, place] for m in range(members)]
        total = [None] * members
        for m in range(members):
            for n in range(m + 1, members):
                term = soft_sign(own[m] - own[n])
                total[m] = term if total[m] is None else total[m] + term
                total[n] = -term if total[n] is None else total[n] - term
        for other in (beside_ref, across_ref):
            for n in range(members):
                value = other[n, v, :, place]
                for m in range(members):
                    total[m] = total[m] + soft_sign(own[m] - value)
        seen = seen_ref[v, :, place]
        for m in range(members):
            out_ref[m, v, :, place] = soft_sign(own[m] - seen) * (1.0 / ensemble) - total[m] * (
                1.0 / (ensemble * (ensemble - 1))
            )
        return carry

    lax.fori_loop(0, variables * tiles, step, 0)


def pair_gradient(own, beside, across, seen, ensemble, moved=1):
    full = pl.BlockSpec(memory_space=pltpu.VMEM)
    return pl.pallas_call(
        functools.partial(pair_kernel, ensemble),
        in_specs=[full] * 4,
        out_specs=full,
        out_shape=jax.ShapeDtypeStruct(own.shape, jnp.float32),
        compiler_params=pltpu.CompilerParams(vmem_limit_bytes=VMEM),
        cost_estimate=pl.CostEstimate(flops=1, bytes_accessed=moved, transcendentals=0),
    )(own, beside, across, seen)


def early_tile(ensemble, own_ref, beside_ref, out_ref):
    members, variables, _, columns = own_ref.shape
    tiles = columns // LANES

    def step(i, carry):
        v = i // tiles
        place = pl.ds(pl.multiple_of((i % tiles) * LANES, LANES), LANES)
        own = [own_ref[m, v, :, place] for m in range(members)]
        total = [None] * members
        for m in range(members):
            for n in range(m + 1, members):
                term = soft_sign(own[m] - own[n])
                total[m] = term if total[m] is None else total[m] + term
                total[n] = -term if total[n] is None else total[n] - term
        for n in range(members):
            value = beside_ref[n, v, :, place]
            for m in range(members):
                total[m] = total[m] + soft_sign(own[m] - value)
        for m in range(members):
            out_ref[m, v, :, place] = total[m]
        return carry

    lax.fori_loop(0, variables * tiles, step, 0)


def mixed_kernel(ensemble, *refs):
    pair_kernel(ensemble, *refs[:4], refs[6])
    early_tile(ensemble, *refs[4:6], refs[7])


def mixed_gradient(mid, near, ensemble):
    full = pl.BlockSpec(memory_space=pltpu.VMEM)
    return pl.pallas_call(
        functools.partial(mixed_kernel, ensemble),
        in_specs=[full] * 6,
        out_specs=[full] * 2,
        out_shape=[jax.ShapeDtypeStruct(tile[0].shape, jnp.float32) for tile in (mid, near)],
        compiler_params=pltpu.CompilerParams(vmem_limit_bytes=VMEM),
        cost_estimate=pl.CostEstimate(flops=1, bytes_accessed=1, transcendentals=0),
    )(*mid, *near)


def later_kernel(ensemble, own_ref, across_ref, part_ref, seen_ref, out_ref):
    members, variables, _, columns = own_ref.shape
    tiles = columns // LANES

    def step(i, carry):
        v = i // tiles
        place = pl.ds(pl.multiple_of((i % tiles) * LANES, LANES), LANES)
        own = [own_ref[m, v, :, place] for m in range(members)]
        total = [part_ref[m, v, :, place] for m in range(members)]
        for n in range(members):
            value = across_ref[n, v, :, place]
            for m in range(members):
                total[m] = total[m] + soft_sign(own[m] - value)
        seen = seen_ref[v, :, place]
        for m in range(members):
            out_ref[m, v, :, place] = soft_sign(own[m] - seen) * (1.0 / ensemble) - total[m] * (
                1.0 / (ensemble * (ensemble - 1))
            )
        return carry

    lax.fori_loop(0, variables * tiles, step, 0)


def later_gradient(own, across, part, seen, ensemble):
    full = pl.BlockSpec(memory_space=pltpu.VMEM)
    return pl.pallas_call(
        functools.partial(later_kernel, ensemble),
        in_specs=[full] * 4,
        out_specs=full,
        out_shape=jax.ShapeDtypeStruct(own.shape, jnp.float32),
        compiler_params=pltpu.CompilerParams(vmem_limit_bytes=VMEM),
        cost_estimate=pl.CostEstimate(flops=1, bytes_accessed=1, transcendentals=0),
    )(own, across, part, seen)


def finish(ensemble, group, own_ref, part_ref, corner_ref):
    own = own_ref[group]
    total = jnp.zeros_like(own)
    for n in range(corner_ref.shape[0]):
        total = total + soft_sign(own - corner_ref[n][None])
    return part_ref[group] - total * (1.0 / (ensemble * (ensemble - 1)))


def spread_lat(edge, mid, band, bands, half, lat_ref):
    group, variables, _, columns = edge.shape
    edge = jnp.where(outside(edge.shape, 2, band, bands, half), 0.0, edge)
    upper = jnp.where(half == 0, edge, mid)
    lower = jnp.where(half == 0, mid, edge)
    grad = jnp.stack([upper, lower], axis=2).reshape(group * variables * NEAR, columns)
    high, low = split(grad)
    return dot(lat_ref[...], jnp.concatenate([high, low, high], axis=0))


def spread_lon(tall, lon_ref, store):
    depth, columns = tall.shape
    tiles = [tall[:, j * LANES : (j + 1) * LANES] for j in range(columns // LANES)]
    lane = lax.broadcasted_iota(jnp.int32, tiles[0].shape, 1)
    zero = jnp.zeros_like(tiles[0])
    count = len(tiles)
    for odd in range(2):
        stacks = []
        for j in range(count):
            if odd:
                after = tiles[j + 1] if j + 1 < count else zero
                near = jnp.where(lane < MARGIN, after, tiles[j])
            else:
                before = tiles[j - 1] if j > 0 else zero
                near = jnp.where(lane >= LANES - MARGIN, before, tiles[j])
            stacks.append(jnp.concatenate(split(near), axis=1))
        stack = jnp.concatenate(stacks, axis=0)
        wide = dot(stack, lon_ref[2 * odd]) + dot(stack, lon_ref[2 * odd + 1])
        for j in range(count):
            store(2 * j + odd, wide[j * depth : (j + 1) * depth])


def spread_kernel(bands, ensemble, first, where_ref, *refs):
    if first:
        edge_trio, mid_trio = refs[:3], refs[3:6]
        lat_ref, lon_ref, out_ref, mid_ref, held, sent = refs[6:]
    else:
        edge_trio, mid_ref = refs[1:4], refs[4]
        lat_ref, lon_ref, out_ref, held, sent = refs[5:]
    band, half = where_ref[0], where_ref[1]
    members = held.shape[0]
    start = pl.multiple_of(half * HALF, HALF)

    def copy(c):
        group = pl.ds(c * GROUP, GROUP)
        return pltpu.make_async_copy(
            held.at[group], out_ref.at[group, :, pl.ds(start, HALF), :], sent.at[c]
        )

    def tall_rows(c):
        group = pl.ds(c * GROUP, GROUP)
        edge = finish(ensemble, group, *edge_trio)
        if first:
            mid = finish(ensemble, group, *mid_trio)
            mid_ref[group] = mid
        else:
            mid = mid_ref[group]
        return spread_lat(edge, mid, band, bands, half, lat_ref)

    chunks = members // GROUP
    after = tall_rows(0)
    for c in range(chunks):
        group = pl.ds(c * GROUP, GROUP)
        tall = after

        def store(k, value, group=group):
            shape = (GROUP, *held.shape[1:3], BLOCK)
            held[group, :, :, k * BLOCK : (k + 1) * BLOCK] = value.reshape(shape)

        if c + 1 < chunks:
            after = tall_rows(c + 1)
        spread_lon(tall, lon_ref, store)
        copy(c).start()
    for c in range(chunks):
        copy(c).wait()


def spread(edge, mid, where, bands, shape, ensemble, moved, out=None):
    members, variables, _, length = shape
    lat = spread_lat_table(GROUP * variables, 64.0 * ensemble)
    lon = spread_lon_table()
    tile = jax.ShapeDtypeStruct(edge[0].shape, jnp.float32)
    whole = jax.ShapeDtypeStruct(shape, jnp.float32)
    full = pl.BlockSpec(memory_space=pltpu.VMEM)
    any_space = pl.BlockSpec(memory_space=pl.ANY)
    first = out is None
    operands = [*edge, *mid] if first else [out, *edge, mid]
    return pl.pallas_call(
        functools.partial(spread_kernel, bands, ensemble, first),
        in_specs=[pl.BlockSpec(memory_space=pltpu.SMEM)]
        + ([full] * 6 if first else [any_space] + [full] * 4)
        + [full] * 2,
        out_specs=[any_space, full] if first else any_space,
        out_shape=[whole, tile] if first else whole,
        scratch_shapes=[
            pltpu.VMEM((members, variables, HALF, length), jnp.float32),
            pltpu.SemaphoreType.DMA((members // GROUP,)),
        ],
        input_output_aliases={} if first else {1: 0},
        compiler_params=pltpu.CompilerParams(vmem_limit_bytes=VMEM),
        cost_estimate=pl.CostEstimate(flops=1, bytes_accessed=moved, transcendentals=0),
    )(where, *operands, jnp.asarray(lat), jnp.asarray(lon))


def swap(value, bit):
    devices = lax.axis_size("member")
    return lax.ppermute(value, "member", [(i, i ^ bit) for i in range(devices)])


def pairs_of(bands, first):
    pairs = [(i, i + 1) for i in range(first, bands - 1, 2)]
    return pairs + [(j, i) for i, j in pairs]


def shards(fields, observed):
    members, _, rows, _ = fields.shape
    bands = lax.axis_size("band")
    ensemble = members * lax.axis_size("member")
    band = lax.axis_index("band").astype(jnp.int32)
    far = jnp.stack([band, band % 2])
    near = jnp.stack([band, 1 - band % 2])
    tie = lax.optimization_barrier
    with jax.named_scope("k_thin"):
        near_part, far_part, mid = thin(fields, observed, band.reshape(1), bands)
    with jax.named_scope("x_near"):
        near_come = lax.ppermute(near_part, "band", pairs_of(bands, 0))
    with jax.named_scope("x_ymid"):
        across_mid = swap(mid, 2)
    with jax.named_scope("x_cmid"):
        beside_mid = swap(mid, 1)
    with jax.named_scope("x_far"):
        far_come = lax.ppermute(far_part, "band", pairs_of(bands, 1))
    near_tile = near_part[:members] + near_come[:members]
    near_seen = near_part[members] + near_come[members]
    with jax.named_scope("x_ynear"):
        across_near = swap(near_tile, 2)
    with jax.named_scope("x_cnear"):
        beside_near = swap(near_tile, 1)
    across_mid, near_tile = tie((across_mid, near_tile))
    with jax.named_scope("x_dmid"):
        corner_mid = swap(across_mid, 1)
    with jax.named_scope("k_pmid"):
        mid_set = (mid, beside_mid, across_mid, observed[:, MARGIN:-MARGIN])
        near_set = (near_tile, beside_near)
        mid_part, near_early = mixed_gradient(mid_set, near_set, ensemble)
    far_come, mid_part = tie((far_come, mid_part))
    far_come, beside_near = tie((far_come, beside_near))
    far_tile = far_part[:members] + far_come[:members]
    far_seen = far_part[members] + far_come[members]
    with jax.named_scope("x_yfar"):
        across_far = swap(far_tile, 2)
    with jax.named_scope("x_cfar"):
        beside_far = swap(far_tile, 1)
    with jax.named_scope("x_dnear"):
        corner_near = swap(across_near, 1)
    with jax.named_scope("k_pnear"):
        near_grad = later_gradient(near_tile, across_near, near_early, near_seen, ensemble)
    trio = (near_tile, near_grad, corner_near)
    with jax.named_scope("k_near"):
        out, mid_grad = spread(trio, (mid, mid_part, corner_mid), near, bands, fields.shape, ensemble, 8000000)
    across_far, out = tie((across_far, out))
    with jax.named_scope("x_dfar"):
        corner_far = swap(across_far, 1)
    with jax.named_scope("k_pfar"):
        far_grad = pair_gradient(far_tile, beside_far, across_far, far_seen, ensemble, 1)
    trio = (far_tile, far_grad, corner_far)
    with jax.named_scope("k_far"):
        out = spread(trio, mid_grad, far, bands, fields.shape, ensemble, 1, out)
    return out


def solution(mesh):
    return jax.shard_map(
        shards,
        mesh=mesh,
        in_specs=(P("member", None, "band", None), P(None, "band", None)),
        out_specs=P("member", None, "band", None),
        check_vma=False,
    )
```
